256 devices in a mesh: dom: 128 (over y, x, z), feat: 2 (over core).
Axes of the slice: x: 4, y: 4, z: 8, core: 2. Of those that a mesh axis runs over, the one named last changes fastest.
Arguments:
- features: bfloat16 [262144, 512], P('dom', 'feat'), may hold values from -6 to 6
- prev_features: bfloat16 [262144, 512], P('dom', 'feat'), may hold values from -6 to 6
- cotangent: bfloat16 [262144, 512], P('dom', 'feat'), may hold values from -6 to 6
- adjacency: bfloat16 [12288, 128, 128], P('dom'), may hold values from -0.21875 to 0.21875
- tile_cols: int32 [12288], P('dom'), may hold values from 0 to 39, as said below
- send_idx: int32 [16384, 24], P('dom'), may hold values from 0 to 2047, as said below
- send_cnt: int32 [16384], P('dom'), may hold values from 0 to 24, as said below
- recv_cnt: int32 [16384], P('dom'), may hold values from 0 to 24, as said below
- stale_grad: bfloat16 [16384, 24, 512], P('dom', None, 'feat'), may hold values from -4 to 4
- w_self: bfloat16 [512, 512], P('feat'), may hold values from -0.1875 to 0.1875
- w_neigh: bfloat16 [512, 512], P('feat'), may hold values from -0.1875 to 0.1875
- layer_bias: float32 [512], P('feat'), may hold values from -4 to 4
Outputs:
- hidden: bfloat16 [262144, 512], P('dom', 'feat')
- input_grad: bfloat16 [262144, 512], P('dom', 'feat')
- boundary_grad: bfloat16 [16384, 24, 512], P('dom', None, 'feat')
The draws below stay inside these ranges and needn't reach their ends.
Inputs may be any that keep to these rules, and one draw needn't show every extreme that they name: `tile_cols`: tile t of a partition lies in row block t // 6; column blocks below 16 are the partition's own rows, the others its received slots. `send_idx`: the indices of one row are distinct. `send_cnt`: A partition sends nothing to itself; some partition receives 24 rows from every other partition. recv_cnt[d * 128 + s] = send_cnt[s * 128 + d].
All inputs are finite; a program needn't handle non-finite values.
Results may differ from the reference program's by a relative error of at most 0.019.
The reference program's roundings to bfloat16 on the way (of `received`, `aggregate`, `pre_grad` and `agg_grad`) count: a program that leaves them out, or rounds other values in their place, can miss the bound.
Values may be sent and summed in bfloat16 or wider, within the bound.
A program may use at most 128 MiB of HBM per device.

```python
import jax
import jax.numpy as jnp
from jax import lax

F = 512
NODES_DEV = 2048
CAP = 24
TPR = 6
ROW_BLOCKS = 16
RECV_BLOCKS = 24
TILES_DEV = 96
NODES = 262144
N_DOM = 128


def count_table(key):
    key = jax.random.fold_in(key, 7)
    level_key, base_key, full_key = jax.random.split(key, 3)
    level = jax.random.randint(level_key, (N_DOM, 1), 1, 5)
    base = jax.random.randint(base_key, (N_DOM, N_DOM), 0, CAP // 2 + 1)
    table = jnp.minimum(base * level, CAP)
    full_dest = jax.random.randint(full_key, (), 0, N_DOM)
    column_ids = jnp.arange(N_DOM, dtype=jnp.int32)
    table = jnp.where(column_ids[None, :] == full_dest, CAP, table)
    table = jnp.where(column_ids[:, None] == column_ids[None, :], 0, table)
    return table.astype(jnp.int32)


def draw_send_cnt(key, part):
    table = count_table(key)
    return table.reshape(-1)


def draw_recv_cnt(key, part):
    table = count_table(key)
    return table.T.reshape(-1)


def draw_send_idx(key, part):
    key = jax.random.fold_in(key, 11)
    scores = jax.random.randint(key, (N_DOM * N_DOM, NODES_DEV), 0, 2 ** 16)
    scores = scores * NODES_DEV + jnp.arange(NODES_DEV, dtype=jnp.int32)[None, :]
    chosen = lax.top_k(scores, CAP)[1]
    return chosen.astype(jnp.int32)


def draw_tile_cols(key, part):
    key = jax.random.fold_in(key, 5)
    coin_key, local_key, remote_key = jax.random.split(key, 3)
    total = N_DOM * ROW_BLOCKS * TPR
    order = jnp.arange(total, dtype=jnp.int32)
    within = order % TPR
    own_block = order // TPR % ROW_BLOCKS
    coin = jax.random.randint(coin_key, (total,), 0, 2)
    local_pick = jax.random.randint(local_key, (total,), 0, ROW_BLOCKS)
    remote_pick = ROW_BLOCKS + jax.random.randint(remote_key, (total,), 0, RECV_BLOCKS)
    chosen = jnp.where(within == 0, own_block, jnp.where(coin == 1, local_pick, remote_pick))
    chosen = chosen.at[total - 1].set(ROW_BLOCKS + RECV_BLOCKS - 1)
    return chosen.astype(jnp.int32)


def steps_of(stream_key, shape, pieces, least, largest):
    loudness, own = 1.0, jax.random.fold_in(stream_key, 6)
    for position, blocks in pieces:
        heights = jnp.exp(jax.random.uniform(jax.random.fold_in(own, position), (blocks,), jnp.float32, least / len(pieces), largest / len(pieces)))
        loudness = loudness * jnp.repeat(heights, shape[position] // blocks).reshape([-1 if axis == position else 1 for axis in range(len(shape))])
    return loudness


def scatter_about(own_key, extent, width, reach, cuts=(), kind=jnp.bfloat16):
    level = steps_of(own_key, extent, cuts, -0.22, 0.18) if cuts else 1.0
    entries = jax.random.normal(own_key, extent, jnp.float32) * width * level
    return jnp.minimum(jnp.maximum(entries, -reach), reach).astype(kind)


def setup_inputs(seed: int = 0) -> dict:
    keys = jax.random.split(jax.random.key(seed), 13)
    features = scatter_about(keys[0], (NODES, F), 1.0, 6.0, ((0, 128), (1, 2)))
    prev_features = scatter_about(keys[1], (NODES, F), 1.0, 6.0, ((0, 128), (1, 2)))
    cotangent = scatter_about(keys[2], (NODES, F), 1.0, 6.0, ((0, 128), (1, 2)))
    adjacency = scatter_about(keys[3], (N_DOM * TILES_DEV, 128, 128), (128 * TPR) ** -0.5, 0.21875, ((0, 128),))
    tile_cols = draw_tile_cols(jax.random.fold_in(keys[12], 71), 0)
    send_idx = draw_send_idx(jax.random.fold_in(keys[12], 71), 0)
    send_cnt = draw_send_cnt(jax.random.fold_in(keys[12], 71), 0)
    recv_cnt = draw_recv_cnt(jax.random.fold_in(keys[12], 71), 0)
    stale_grad = scatter_about(keys[8], (N_DOM * N_DOM, CAP, F), 0.5, 4.0, ((0, 128), (2, 2)))
    w_self = scatter_about(keys[9], (F, F), (2 * F) ** -0.5, 0.1875, ((0, 2),))
    w_neigh = scatter_about(keys[10], (F, F), (2 * F) ** -0.5, 0.1875, ((0, 2),))
    layer_bias = scatter_about(keys[11], (F,), 1.0, 4.0, ((0, 2),), jnp.float32)
    return dict(features=features, prev_features=prev_features, cotangent=cotangent, adjacency=adjacency, tile_cols=tile_cols, send_idx=send_idx, send_cnt=send_cnt, recv_cnt=recv_cnt, stale_grad=stale_grad, w_self=w_self, w_neigh=w_neigh, layer_bias=layer_bias)


def partition_pass(local_rows, incoming, grad_rows, tile_block, column_ids, returned, index_table, sent_counts, taken_counts, w_self, w_neigh, layer_bias):
    combined = jnp.concatenate([local_rows, incoming], axis=0).reshape(ROW_BLOCKS + RECV_BLOCKS, 128, F)
    picked = combined[column_ids].reshape(ROW_BLOCKS, TPR, 128, F).astype(jnp.float32)
    square_tiles = tile_block.reshape(ROW_BLOCKS, TPR, 128, 128).astype(jnp.float32)
    aggregate = jnp.einsum("rtij,rtjf->rif", square_tiles, picked).reshape(NODES_DEV, F).astype(jnp.bfloat16)
    preact = jnp.dot(local_rows, w_self, preferred_element_type=jnp.float32)
    preact = preact + jnp.dot(aggregate, w_neigh, preferred_element_type=jnp.float32) + layer_bias
    hidden = jnp.maximum(preact, 0.0).astype(jnp.bfloat16)
    pre_grad = jnp.where(preact > 0, grad_rows.astype(jnp.float32), 0.0).astype(jnp.bfloat16)
    self_grad = jnp.dot(pre_grad, w_self.T, preferred_element_type=jnp.float32)
    agg_grad = jnp.dot(pre_grad, w_neigh.T, preferred_element_type=jnp.float32).astype(jnp.bfloat16)
    terms = jnp.einsum("rtij,rif->rtjf", square_tiles, agg_grad.reshape(ROW_BLOCKS, 128, F).astype(jnp.float32))
    comb_grad = jnp.zeros((ROW_BLOCKS + RECV_BLOCKS, 128, F), jnp.float32).at[column_ids].add(terms.reshape(TILES_DEV, 128, F))
    slot_ids = jnp.arange(CAP, dtype=jnp.int32)
    send_valid = (slot_ids[None, :] < sent_counts[:, None])[..., None]
    back_rows = jnp.where(send_valid, returned.astype(jnp.float32), 0.0)
    total_grad = self_grad + comb_grad[:ROW_BLOCKS].reshape(NODES_DEV, F)
    total_grad = total_grad.at[index_table.reshape(-1)].add(back_rows.reshape(-1, F))
    take_valid = (slot_ids[None, :] < taken_counts[:, None])[..., None]
    fresh_grad = jnp.where(take_valid, comb_grad[ROW_BLOCKS:].reshape(N_DOM, CAP, F), 0.0).astype(jnp.bfloat16)
    return hidden, total_grad.astype(jnp.bfloat16), fresh_grad


def reference(features, prev_features, cotangent, adjacency, tile_cols, send_idx, send_cnt, recv_cnt, stale_grad, w_self, w_neigh, layer_bias):
    local_all = features.reshape(N_DOM, NODES_DEV, F)
    prev_all = prev_features.reshape(N_DOM, NODES_DEV, F)
    index_all = send_idx.reshape(N_DOM, N_DOM, CAP)
    count_all = send_cnt.reshape(N_DOM, N_DOM)
    taken_all = recv_cnt.reshape(N_DOM, N_DOM)
    slot_ids = jnp.arange(CAP, dtype=jnp.int32)
    sent_rows = jax.vmap(lambda source, order: source[order])(prev_all, index_all)
    valid_slots = (slot_ids[None, None, :] < count_all[:, :, None])[..., None]
    sent_rows = jnp.where(valid_slots, sent_rows, jnp.zeros((), jnp.bfloat16))
    received = jnp.swapaxes(sent_rows, 0, 1).reshape(N_DOM, N_DOM * CAP, F)
    returned = jnp.swapaxes(stale_grad.reshape(N_DOM, N_DOM, CAP, F), 0, 1)
    grad_all = cotangent.reshape(N_DOM, NODES_DEV, F)
    tiles_all = adjacency.reshape(N_DOM, TILES_DEV, 128, 128)
    cols_all = tile_cols.reshape(N_DOM, TILES_DEV)

    def one_partition(packed):
        return partition_pass(packed[0], packed[1], packed[2], packed[3], packed[4], packed[5], packed[6], packed[7], packed[8], w_self, w_neigh, layer_bias)

    hidden, input_grad, boundary_grad = lax.map(one_partition, (local_all, received, grad_all, tiles_all, cols_all, returned, index_all, count_all, taken_all))
    return hidden.reshape(NODES, F), input_grad.reshape(NODES, F), boundary_grad.reshape(N_DOM * N_DOM, CAP, F)
```

```python
import functools

import jax
import jax.numpy as jnp
from jax import lax
from jax.experimental import pallas as pl
from jax.experimental.pallas import tpu as pltpu
from jax.sharding import PartitionSpec as P

MESH = pl.DeviceIdType.MESH
PEERS = 128
CAP = 24
GROUP = 16
GROUPS = PEERS // GROUP
SLOTS = GROUP * CAP


def offset_peer(me, i):
    z, x, y = lax.rem(me, 8), lax.rem(me // 8, 4), me // 32
    dz, dx, dy = lax.rem(i, 8), lax.rem(i // 8, 4), i // 32
    return (lax.rem(y + dy, 4) * 4 + lax.rem(x + dx, 4)) * 8 + lax.rem(z + dz, 8)


def exchange_kernel(idx_ref, cnt_ref, prev_ref, stale_ref, recv_ref, back_ref, out_buf, send_sem, recv_sem, local_sem):
    me, feat = lax.axis_index("dom"), lax.axis_index("feat")
    rows = prev_ref.shape[0]
    barrier = pltpu.get_barrier_semaphore()

    def greet(i, carry):
        pl.semaphore_signal(
            barrier, inc=1, device_id=(offset_peer(me, i), feat), device_id_type=MESH
        )
        return carry

    lax.fori_loop(1, PEERS, greet, 0)
    own = pltpu.make_async_copy(stale_ref.at[me], back_ref.at[me], local_sem)
    own.start()
    slot_of = lax.broadcasted_iota(jnp.int32, (CAP, PEERS), 0)
    idx = jnp.where(slot_of < cnt_ref[...], idx_ref[...], -1).astype(jnp.float32)
    tiled = jnp.concatenate([idx] * GROUP, axis=0)
    lane = lax.broadcasted_iota(jnp.int32, (SLOTS, PEERS), 1)
    place = lax.broadcasted_iota(jnp.int32, (GROUP, CAP, PEERS), 0).reshape(SLOTS, PEERS)
    node = lax.broadcasted_iota(jnp.int32, (SLOTS, rows), 1)

    def gather(g, carry):
        i = g * GROUP + place
        dz, dx, dy = i & 7, (i >> 3) & 3, i >> 5
        z, x, y = me & 7, (me >> 3) & 3, me >> 5
        dest = (((y + dy) & 3) * 4 + ((x + dx) & 3)) * 8 + ((z + dz) & 7)
        column = jnp.sum(jnp.where(lane == dest, tiled, 0.0), axis=1, keepdims=True)
        pick = (node == column.astype(jnp.int32)).astype(jnp.float32).astype(jnp.bfloat16)
        sent = jnp.dot(pick, prev_ref[...], preferred_element_type=jnp.float32)
        out_buf[pl.ds(g * GROUP, GROUP)] = sent.reshape(GROUP, CAP, -1).astype(jnp.bfloat16)

        @pl.when(g == 0)
        def _():
            pl.semaphore_wait(barrier, PEERS - 1)

        def send(i, carry):
            peer = offset_peer(me, i)
            pltpu.make_async_remote_copy(
                src_ref=out_buf.at[i],
                dst_ref=recv_ref.at[me],
                send_sem=send_sem.at[0],
                recv_sem=recv_sem.at[0],
                device_id=(peer, feat),
                device_id_type=MESH,
            ).start()
            return carry

        lax.fori_loop(jnp.maximum(g * GROUP, 1), (g + 1) * GROUP, send, 0)
        return carry

    lax.fori_loop(0, GROUPS, gather, 0)

    def send_back(i, carry):
        peer = offset_peer(me, i)
        pltpu.make_async_remote_copy(
            src_ref=stale_ref.at[peer],
            dst_ref=back_ref.at[me],
            send_sem=send_sem.at[1],
            recv_sem=recv_sem.at[1],
            device_id=(peer, feat),
            device_id_type=MESH,
        ).start()
        return carry

    lax.fori_loop(1, PEERS, send_back, 0)
    own.wait()
    own = pltpu.make_async_copy(out_buf.at[0], recv_ref.at[me], local_sem)
    own.start()
    own.wait()
    rest = pl.ds(0, PEERS - 1)
    for a, ref in enumerate((recv_ref, back_ref)):
        pltpu.make_async_copy(ref.at[rest], ref.at[rest], recv_sem.at[a]).wait()
        pltpu.make_async_copy(ref.at[rest], ref.at[rest], send_sem.at[a]).wait()


def exchange(send_idx, send_cnt, prev_features, stale_grad):
    width = prev_features.shape[1]
    shape = jax.ShapeDtypeStruct((PEERS, CAP, width), jnp.bfloat16)
    vmem = pl.BlockSpec(memory_space=pltpu.VMEM)
    anywhere = pl.BlockSpec(memory_space=pl.ANY)
    return pl.pallas_call(
        exchange_kernel,
        out_shape=[shape, shape],
        in_specs=[vmem, vmem, vmem, anywhere],
        out_specs=[anywhere, anywhere],
        scratch_shapes=[
            pltpu.VMEM((PEERS, CAP, width), jnp.bfloat16),
            pltpu.SemaphoreType.DMA((2,)),
            pltpu.SemaphoreType.DMA((2,)),
            pltpu.SemaphoreType.DMA,
        ],
        compiler_params=pltpu.CompilerParams(
            collective_id=0, has_side_effects=True, vmem_limit_bytes=48 << 20
        ),
    )(send_idx.T, send_cnt.reshape(1, PEERS), prev_features, stale_grad)


def per_device(
    features,
    prev_features,
    cotangent,
    adjacency,
    tile_cols,
    send_idx,
    send_cnt,
    recv_cnt,
    stale_grad,
    w_self,
    w_neigh,
    layer_bias,
):
    peer_count = lax.axis_size("dom")
    rows_dev, shard_width = features.shape
    capacity = send_idx.shape[1]
    row_blocks = rows_dev // 128
    per_row = adjacency.shape[0] // row_blocks
    slot_ids = jnp.arange(capacity, dtype=jnp.int32)
    send_valid = slot_ids[None, :] < send_cnt[:, None]
    row_ids = jnp.arange(rows_dev, dtype=jnp.int32)
    sender = (send_idx.reshape(-1)[:, None] == row_ids[None, :]) & send_valid.reshape(-1)[:, None]
    sender = sender.astype(jnp.bfloat16)
    incoming, returned = exchange(send_idx, send_cnt, prev_features, stale_grad)
    combined = jnp.concatenate(
        [features, incoming.reshape(peer_count * capacity, shard_width)], axis=0
    )
    blocks = combined.reshape(-1, 128, shard_width)
    block_count = blocks.shape[0]
    block_ids = jnp.arange(block_count, dtype=jnp.int32)
    selector = tile_cols[:, None] == block_ids[None, :]
    select_half = selector.astype(jnp.bfloat16)
    picked = jnp.einsum(
        "tc,cjf->tjf", select_half, blocks, preferred_element_type=jnp.float32
    ).astype(jnp.bfloat16)
    picked = picked.reshape(row_blocks, per_row, 128, shard_width)
    square_tiles = adjacency.reshape(row_blocks, per_row, 128, 128)
    aggregate = jnp.einsum(
        "rtij,rtjf->rif", square_tiles, picked, preferred_element_type=jnp.float32
    )
    aggregate = aggregate.reshape(rows_dev, shard_width).astype(jnp.bfloat16)
    partial_sum = jnp.dot(features, w_self, preferred_element_type=jnp.float32)
    partial_sum = partial_sum + jnp.dot(aggregate, w_neigh, preferred_element_type=jnp.float32)
    preact = lax.psum_scatter(partial_sum, "feat", scatter_dimension=1, tiled=True) + layer_bias
    hidden = jnp.maximum(preact, 0.0).astype(jnp.bfloat16)
    pre_grad = jnp.where(preact > 0, cotangent.astype(jnp.float32), 0.0).astype(jnp.bfloat16)
    contract = (((1,), (1,)), ((), ()))
    portion = lax.all_gather(pre_grad, "feat", axis=1, tiled=True)
    self_term = lax.dot_general(portion, w_self, contract, preferred_element_type=jnp.float32)
    neigh_term = lax.dot_general(portion, w_neigh, contract, preferred_element_type=jnp.float32)
    agg_grad = neigh_term.astype(jnp.bfloat16).reshape(row_blocks, 128, shard_width)
    terms = jnp.einsum("rtij,rif->rtjf", square_tiles, agg_grad, preferred_element_type=jnp.float32)
    select_full = selector.astype(jnp.float32)
    comb_grad = jnp.einsum(
        "tc,tjf->cjf",
        select_full,
        terms.reshape(-1, 128, shard_width),
        precision=lax.Precision.HIGHEST,
    )
    back_flat = returned.reshape(-1, shard_width)
    back_sum = lax.dot_general(
        sender, back_flat, (((0,), (0,)), ((), ())), preferred_element_type=jnp.float32
    )
    total_grad = self_term + comb_grad[:row_blocks].reshape(rows_dev, shard_width) + back_sum
    take_valid = (slot_ids[None, :] < recv_cnt[:, None])[..., None]
    fresh_grad = jnp.where(
        take_valid, comb_grad[row_blocks:].reshape(peer_count, capacity, shard_width), 0.0
    )
    return (hidden, total_grad.astype(jnp.bfloat16), fresh_grad.astype(jnp.bfloat16))


def solution(mesh):
    return jax.shard_map(
        per_device,
        mesh=mesh,
        in_specs=(
            P("dom", "feat"),
            P("dom", "feat"),
            P("dom", "feat"),
            P("dom", None, None),
            P("dom"),
            P("dom", None),
            P("dom"),
            P("dom"),
            P("dom", None, "feat"),
            P("feat", None),
            P("feat", None),
            P("feat"),
        ),
        out_specs=(P("dom", "feat"), P("dom", "feat"), P("dom", None, "feat")),
        check_vma=False,
    )
```

```python
import jax
import jax.numpy as jnp
from jax import lax
from jax.experimental import pallas as pl
from jax.experimental.pallas import tpu as pltpu
from jax.sharding import PartitionSpec as P

MESH = pl.DeviceIdType.MESH
BF16, F32 = jnp.bfloat16, jnp.float32
PEERS = 128
CAP = 24
GROUP = 16
GROUPS = PEERS // GROUP
SLOTS = GROUP * CAP
BLOCK = 128
GROUP_BLOCKS = SLOTS // BLOCK
TPR = 6
CHUNKS = 4
PIECE = 256
CONTRACT_LAST = (((1,), (1,)), ((), ()))
CONTRACT_FIRST = (((0,), (0,)), ((), ()))


def ahead(me, i):
    z, x, y = lax.rem(me, 8), lax.rem(me // 8, 4), me // 32
    dz, dx, dy = lax.rem(i, 8), lax.rem(i // 8, 4), i // 32
    return (lax.rem(y + dy, 4) * 4 + lax.rem(x + dx, 4)) * 8 + lax.rem(z + dz, 8)


def behind(me, i):
    z, x, y = lax.rem(me, 8), lax.rem(me // 8, 4), me // 32
    dz, dx, dy = lax.rem(i, 8), lax.rem(i // 8, 4), i // 32
    return (lax.rem(y + 4 - dy, 4) * 4 + lax.rem(x + 4 - dx, 4)) * 8 + lax.rem(z + 8 - dz, 8)


def layer_kernel(
    tile_ref,
    idx_ref,
    cnt_ref,
    taken_ref,
    bias_ref,
    feat_ref,
    prev_ref,
    cot_ref,
    adj_ref,
    stale_ref,
    ws_ref,
    wn_ref,
    hid_ref,
    grad_ref,
    bnd_ref,
    prev,
    comb,
    feat2,
    cot,
    ws,
    wn,
    bias,
    adj,
    out_buf,
    recv,
    back,
    agg,
    agg2,
    agg_grad,
    total,
    terms,
    sums,
    spread,
    rows_of,
    meta_v,
    meta_s,
    load_sem,
    send_sem,
    recv_sem,
    back_sem,
    pair_send,
    pair_recv,
    out_sem,
):
    me, feat = lax.axis_index("dom"), lax.axis_index("feat")
    nodes = prev.shape[0]
    chunk = nodes // CHUNKS
    blocks = nodes // BLOCK
    barrier = pltpu.get_barrier_semaphore()

    def greet(i, carry):
        pl.semaphore_signal(barrier, inc=1, device_id=(ahead(me, i), feat), device_id_type=MESH)
        return carry

    pl.semaphore_signal(barrier, inc=1, device_id=(me, 1 - feat), device_id_type=MESH)
    lax.fori_loop(1, PEERS, greet, 0)

    loads = [
        pltpu.make_async_copy(src, dst, load_sem.at[n])
        for n, (src, dst) in enumerate(
            (
                (prev_ref, prev),
                (feat_ref, comb.at[pl.ds(0, blocks)]),
                (adj_ref, adj),
                (cot_ref, cot.at[feat]),
                (ws_ref, ws.at[0]),
                (wn_ref, wn.at[0]),
                (stale_ref.at[me], back.at[0]),
            )
        )
    ]
    for load in loads:
        load.start()
    bias[feat] = jnp.broadcast_to(bias_ref[...], bias.shape[1:])

    slot_of = lax.broadcasted_iota(jnp.int32, (CAP, PEERS), 0)
    idx = jnp.where(slot_of < cnt_ref[...], idx_ref[...], -1).astype(F32)
    tiled = jnp.concatenate([idx] * GROUP, axis=0)
    lane = lax.broadcasted_iota(jnp.int32, (SLOTS, PEERS), 1)
    place = lax.broadcasted_iota(jnp.int32, (GROUP, CAP, PEERS), 0).reshape(SLOTS, PEERS)
    node = lax.broadcasted_iota(jnp.int32, (SLOTS, nodes), 1)
    loads[0].wait()

    def gather(g, carry):
        i = g * GROUP + place
        dz, dx, dy = i & 7, (i >> 3) & 3, i >> 5
        z, x, y = me & 7, (me >> 3) & 3, me >> 5
        dest = (((y + dy) & 3) * 4 + ((x + dx) & 3)) * 8 + ((z + dz) & 7)
        column = jnp.sum(jnp.where(lane == dest, tiled, 0.0), axis=1, keepdims=True)
        pick = (node == column.astype(jnp.int32)).astype(F32).astype(BF16)
        sent = jnp.dot(pick, prev[...], preferred_element_type=F32)
        out_buf[pl.ds(g * GROUP, GROUP)] = sent.reshape(GROUP, CAP, -1).astype(BF16)
        rows_of[g] = jnp.transpose(jnp.broadcast_to(column, (SLOTS, PEERS)))[:8]

        @pl.when(g == 0)
        def _():
            pl.semaphore_wait(barrier, PEERS)

        def send(i, carry):
            pltpu.make_async_remote_copy(
                src_ref=out_buf.at[i],
                dst_ref=recv.at[me],
                send_sem=send_sem.at[0],
                recv_sem=recv_sem,
                device_id=(ahead(me, i), feat),
                device_id_type=MESH,
            ).start()
            return carry

        lax.fori_loop(jnp.maximum(g * GROUP, 1), (g + 1) * GROUP, send, 0)
        return carry

    lax.fori_loop(0, GROUPS, gather, 0)
    recv[me] = out_buf[0]

    def to_pair(n, src, dst):
        return pltpu.make_async_remote_copy(
            src_ref=src,
            dst_ref=dst,
            send_sem=pair_send.at[n],
            recv_sem=pair_recv.at[n],
            device_id=(me, 1 - feat),
            device_id_type=MESH,
        )

    pairs = [
        to_pair(CHUNKS, ws_ref, ws.at[1]),
        to_pair(CHUNKS + 1, wn_ref, wn.at[1]),
        to_pair(CHUNKS + 2, bias.at[feat], bias.at[feat]),
        to_pair(CHUNKS + 3, feat_ref, feat2),
        to_pair(CHUNKS + 4, cot_ref, cot.at[feat]),
    ]
    for pair in pairs:
        pair.start()

    def send_back(i, carry):
        peer = behind(me, i)
        pltpu.make_async_remote_copy(
            src_ref=stale_ref.at[peer],
            dst_ref=back.at[i],
            send_sem=send_sem.at[1],
            recv_sem=back_sem.at[i // GROUP],
            device_id=(peer, feat),
            device_id_type=MESH,
        ).start()
        return carry

    lax.fori_loop(1, PEERS, send_back, 0)

    sub = lax.broadcasted_iota(jnp.int32, (BLOCK, BLOCK), 0)
    lanes = lax.broadcasted_iota(jnp.int32, (BLOCK, BLOCK), 1)
    tiles = adj.shape[0]

    def spread_cols(t, carry):
        down, across = carry
        col = tile_ref[t]
        return jnp.where(sub == t, col, down), jnp.where(lanes == t, col, across)

    def count(hits, axis=0):
        return jnp.sum(jnp.where(hits, 1, 0), axis=axis, keepdims=True)

    far = jnp.full((BLOCK, BLOCK), 1000, jnp.int32)
    down, across = lax.fori_loop(0, tiles, spread_cols, (far, far))
    rank = count(across * BLOCK + lanes < down * BLOCK + sub, axis=1)
    at_rank = jnp.where(lanes == rank, 1, 0)
    follows = jnp.where(lanes == rank + 1, 1, 0)
    col_here = jnp.sum(down * at_rank, axis=0, keepdims=True)
    col_before = jnp.sum((down + 1) * follows, axis=0, keepdims=True)
    meta_v[...] = jnp.zeros(meta_v.shape, jnp.int32)
    meta_v[0:1, :] = jnp.sum(sub * at_rank, axis=0, keepdims=True)
    meta_v[1:2, :] = jnp.where(col_here + 1 == col_before, 1, 0)
    meta_v[2:3, :] = jnp.maximum(count(down <= lanes) - 1, 0)
    meta_v[3:4, :] = jnp.minimum(count(down == lanes), 1)
    meta_copy = pltpu.make_async_copy(meta_v, meta_s, out_sem.at[3])
    meta_copy.start()
    meta_copy.wait()

    all_but_one = pl.ds(0, PEERS - 1)
    for load in loads[1:]:
        load.wait()
    pltpu.make_async_copy(recv.at[all_but_one], recv.at[all_but_one], recv_sem).wait()

    def place_rows(g, carry):
        rows = recv[pl.ds(g * GROUP, GROUP)].astype(F32).reshape(SLOTS, -1).astype(BF16)
        comb[pl.ds(blocks + g * GROUP_BLOCKS, GROUP_BLOCKS)] = rows.reshape(GROUP_BLOCKS, BLOCK, -1)
        return carry

    lax.fori_loop(0, GROUPS, place_rows, 0)

    def rows_of_chunk(q):
        return pl.ds(pl.multiple_of(q * chunk, chunk), chunk)

    def agg_pair(q):
        return to_pair(q, agg.at[rows_of_chunk(q)], agg2.at[rows_of_chunk(q)])

    def aggregate(q, carry):
        def row_block(r, carry):
            left = jnp.concatenate([adj[r * TPR + j] for j in range(TPR)], axis=1)
            right = jnp.concatenate(
                [comb[tile_ref[r * TPR + j]] for j in range(TPR)], axis=0
            )
            summed = jnp.dot(left, right, preferred_element_type=F32)
            agg[pl.ds(pl.multiple_of(r * BLOCK, BLOCK), BLOCK)] = summed.astype(BF16)
            return carry

        per_chunk = chunk // BLOCK
        lax.fori_loop(q * per_chunk, (q + 1) * per_chunk, row_block, 0)
        agg_pair(q).start()
        return carry

    lax.fori_loop(0, CHUNKS, aggregate, 0)
    for pair in pairs:
        pair.wait()

    def dense(q, carry):
        agg_pair(q).wait()
        rows = rows_of_chunk(q)
        own = comb[pl.ds(q * (chunk // BLOCK), chunk // BLOCK)].reshape(chunk, -1)
        other = feat2[pl.ds(q * (chunk // BLOCK), chunk // BLOCK)].reshape(chunk, -1)
        neigh_grad = self_grad = None
        for j in range(2):
            cols = slice(j * 256, (j + 1) * 256)
            preact = jnp.dot(own, ws[0, :, cols], preferred_element_type=F32)
            preact += jnp.dot(other, ws[1, :, cols], preferred_element_type=F32)
            preact += jnp.dot(agg[rows, :], wn[0, :, cols], preferred_element_type=F32)
            preact += jnp.dot(agg2[rows, :], wn[1, :, cols], preferred_element_type=F32)
            preact += bias[j][0:1, :]
            pre_grad = jnp.where(preact > 0, cot[j, rows, :].astype(F32), 0.0).astype(BF16)
            cot[j, rows, :] = jnp.maximum(preact, 0.0).astype(BF16)
            part = lax.dot_general(
                pre_grad, wn[0, :, cols], CONTRACT_LAST, preferred_element_type=F32
            )
            neigh_grad = part if j == 0 else neigh_grad + part
            part = lax.dot_general(
                pre_grad, ws[0, :, cols], CONTRACT_LAST, preferred_element_type=F32
            )
            self_grad = part if j == 0 else self_grad + part
        agg_grad[rows, :] = neigh_grad.astype(BF16)
        total[rows, :] = self_grad
        return carry

    lax.fori_loop(0, CHUNKS, dense, 0)
    hid_copy = pltpu.make_async_copy(cot.at[feat], hid_ref, out_sem.at[0])
    hid_copy.start()

    def tile_terms(r, carry):
        left = jnp.concatenate([adj[r * TPR + j] for j in range(TPR)], axis=1)
        right = agg_grad[pl.ds(pl.multiple_of(r * BLOCK, BLOCK), BLOCK), :]
        part = lax.dot_general(left, right, CONTRACT_FIRST, preferred_element_type=F32)
        terms[pl.ds(r * TPR, TPR)] = part.reshape(TPR, BLOCK, -1)
        return carry

    lax.fori_loop(0, blocks, tile_terms, 0)

    def running(i, carry):
        carry = carry * meta_s[1, i].astype(F32) + terms[meta_s[0, i]]
        sums[i] = carry
        return carry

    lax.fori_loop(0, tiles, running, jnp.zeros(terms.shape[1:], F32))

    def column_sum(c):
        return sums[meta_s[2, c]] * meta_s[3, c].astype(F32)

    def add_local(c, carry):
        rows = pl.ds(pl.multiple_of(c * BLOCK, BLOCK), BLOCK)
        total[rows, :] += column_sum(c)
        return carry

    lax.fori_loop(0, blocks, add_local, 0)

    pltpu.make_async_copy(out_buf.at[all_but_one], out_buf.at[all_but_one], send_sem.at[0]).wait()
    slot = lax.broadcasted_iota(jnp.int32, (GROUP, CAP, 256), 1).reshape(SLOTS, 256).astype(F32)
    taken = jnp.broadcast_to(taken_ref[...].astype(F32), (SLOTS, PEERS))

    def boundary(g, carry):
        first = blocks + g * GROUP_BLOCKS
        rows = jnp.concatenate([column_sum(first + n) for n in range(GROUP_BLOCKS)], axis=0)
        limit = jnp.sum(
            jnp.where(lane == g * GROUP + place, taken, 0.0), axis=1, keepdims=True
        )
        rows = jnp.where(slot < limit, rows, 0.0)
        out_buf[pl.ds(g * GROUP, GROUP)] = rows.reshape(GROUP, CAP, -1).astype(BF16)
        return carry

    lax.fori_loop(0, GROUPS, boundary, 0)
    bnd_copy = pltpu.make_async_copy(out_buf, bnd_ref, out_sem.at[1])
    bnd_copy.start()

    def scatter(g, first):
        row = rows_of[g][0:1, :]

        def mark(p, carry):
            at = lax.broadcasted_iota(jnp.int32, (PIECE, SLOTS), 0) + p * PIECE
            hit = jnp.where(at.astype(F32) == row, 1.0, 0.0)
            spread[pl.ds(pl.multiple_of(p * PIECE, PIECE), PIECE), :] = hit.astype(BF16)
            return carry

        lax.fori_loop(0, nodes // PIECE, mark, 0)
        arrived = back.at[pl.ds(0, GROUP - first)]
        pltpu.make_async_copy(arrived, arrived, back_sem.at[g]).wait()
        values = back[pl.ds(g * GROUP, GROUP)].astype(F32).reshape(SLOTS, -1).astype(BF16)

        def add(p, carry):
            rows = pl.ds(pl.multiple_of(p * PIECE, PIECE), PIECE)
            total[rows, :] += jnp.dot(spread[rows, :], values, preferred_element_type=F32)
            return carry

        lax.fori_loop(0, nodes // PIECE, add, 0)

    scatter(0, 1)

    def scatter_group(g, carry):
        scatter(g, 0)
        return carry

    lax.fori_loop(1, GROUPS, scatter_group, 0)
    prev[...] = total[...].astype(BF16)
    grad_copy = pltpu.make_async_copy(prev, grad_ref, out_sem.at[2])
    grad_copy.start()
    pltpu.make_async_copy(back.at[all_but_one], back.at[all_but_one], send_sem.at[1]).wait()
    hid_copy.wait()
    bnd_copy.wait()
    grad_copy.wait()


def per_device(
    features,
    prev_features,
    cotangent,
    adjacency,
    tile_cols,
    send_idx,
    send_cnt,
    recv_cnt,
    stale_grad,
    w_self,
    w_neigh,
    layer_bias,
):
    nodes, width = features.shape
    tiles = adjacency.shape[0]
    rows = jax.ShapeDtypeStruct((nodes, width), BF16)
    slots = jax.ShapeDtypeStruct((PEERS, CAP, width), BF16)
    anywhere = pl.BlockSpec(memory_space=pl.ANY)
    vmem = pl.BlockSpec(memory_space=pltpu.VMEM)
    smem = pl.BlockSpec(memory_space=pltpu.SMEM)
    dma = pltpu.SemaphoreType.DMA
    whole = pltpu.VMEM((nodes, width), BF16)
    return pl.pallas_call(
        layer_kernel,
        out_shape=[rows, rows, slots],
        in_specs=[smem] + [vmem] * 4 + [anywhere] * 7,
        out_specs=[anywhere] * 3,
        scratch_shapes=[
            whole,
            pltpu.VMEM((nodes // BLOCK + GROUPS * GROUP_BLOCKS, BLOCK, width), BF16),
            pltpu.VMEM((nodes // BLOCK, BLOCK, width), BF16),
            pltpu.VMEM((2, nodes, width), BF16),
            pltpu.VMEM((2,) + w_self.shape, BF16),
            pltpu.VMEM((2,) + w_neigh.shape, BF16),
            pltpu.VMEM((2, 8, width), F32),
            pltpu.VMEM(adjacency.shape, BF16),
            pltpu.VMEM((PEERS, CAP, width), BF16),
            pltpu.VMEM((PEERS, CAP, width), BF16),
            pltpu.VMEM((PEERS, CAP, width), BF16),
            whole,
            whole,
            whole,
            pltpu.VMEM((nodes, width), F32),
            pltpu.VMEM((tiles, BLOCK, width), F32),
            pltpu.VMEM((tiles, BLOCK, width), F32),
            pltpu.VMEM((nodes, SLOTS), BF16),
            pltpu.VMEM((GROUPS, 8, SLOTS), F32),
            pltpu.VMEM((8, BLOCK), jnp.int32),
            pltpu.SMEM((8, BLOCK), jnp.int32),
            dma((7,)),
            dma((2,)),
            dma,
            dma((GROUPS,)),
            dma((CHUNKS + 5,)),
            dma((CHUNKS + 5,)),
            dma((4,)),
        ],
        compiler_params=pltpu.CompilerParams(
            collective_id=0, has_side_effects=True, vmem_limit_bytes=62 << 20
        ),
    )(
        tile_cols,
        send_idx.T,
        send_cnt.reshape(1, PEERS),
        recv_cnt.reshape(1, PEERS),
        layer_bias.reshape(1, width),
        features.reshape(nodes // BLOCK, BLOCK, width),
        prev_features,
        cotangent,
        adjacency,
        stale_grad,
        w_self,
        w_neigh,
    )


def solution(mesh):
    return jax.shard_map(
        per_device,
        mesh=mesh,
        in_specs=(
            P("dom", "feat"),
            P("dom", "feat"),
            P("dom", "feat"),
            P("dom", None, None),
            P("dom"),
            P("dom", None),
            P("dom"),
            P("dom"),
            P("dom", None, "feat"),
            P("feat", None),
            P("feat", None),
            P("feat"),
        ),
        out_specs=(P("dom", "feat"), P("dom", "feat"), P("dom", None, "feat")),
        check_vma=False,
    )
```

```python
import jax
import jax.numpy as jnp
from jax import lax
from jax.experimental import pallas as pl
from jax.experimental.pallas import tpu as pltpu
from jax.sharding import PartitionSpec as P

MESH = pl.DeviceIdType.MESH
BF16, F32 = jnp.bfloat16, jnp.float32
PEERS = 128
CAP = 24
GROUP = 16
GROUPS = PEERS // GROUP
SLOTS = GROUP * CAP
BLOCK = 128
GROUP_BLOCKS = SLOTS // BLOCK
TPR = 6
CHUNKS = 4
PARTS = 2
PIECE = 256
CONTRACT_LAST = (((1,), (1,)), ((), ()))
CONTRACT_FIRST = (((0,), (0,)), ((), ()))


def torus(me, sign):
    z, x, y = lax.rem(me, 8), lax.rem(me // 8, 4), me // 32

    def column(c):
        dy, dx = c // 4, lax.rem(c, 4)
        if sign < 0:
            dy, dx = 4 - dy, 4 - dx
        return (lax.rem(y + dy, 4) * 4 + lax.rem(x + dx, 4)) * 8

    return column, [lax.rem(z + 8 + sign * dz, 8) for dz in range(8)]


def layer_kernel(
    tile_hbm,
    idx_hbm,
    cnt_hbm,
    taken_hbm,
    bias_hbm,
    feat_ref,
    prev_ref,
    cot_ref,
    adj_ref,
    stale_ref,
    ws_ref,
    wn_ref,
    hid_ref,
    grad_ref,
    bnd_ref,
    tile_ref,
    idx_ref,
    cnt_ref,
    taken_ref,
    bias_ref,
    prev,
    comb,
    feat2,
    cot,
    ws,
    wn,
    bias,
    adj,
    out_buf,
    recv,
    back,
    agg,
    agg2,
    agg_grad,
    total,
    terms,
    sums,
    spread,
    rows_of,
    meta_v,
    meta_s,
    load_sem,
    send_sem,
    recv_sem,
    back_sem,
    pair_send,
    pair_recv,
    out_sem,
):
    me, feat = lax.axis_index("dom"), lax.axis_index("feat")
    nodes = prev.shape[0]
    chunk = nodes // CHUNKS
    blocks = nodes // BLOCK
    barrier = pltpu.get_barrier_semaphore()

    column_ahead, z_ahead = torus(me, 1)
    column_behind, z_behind = torus(me, -1)

    def greet(c, carry):
        base = column_ahead(c)
        for dz in range(8):
            pl.semaphore_signal(
                barrier, inc=1, device_id=(base + z_ahead[dz], feat), device_id_type=MESH
            )
        return carry

    loads = [
        pltpu.make_async_copy(src, dst, load_sem.at[n])
        for n, (src, dst) in enumerate(
            (
                (prev_ref, prev),
                (idx_hbm, idx_ref),
                (cnt_hbm, cnt_ref),
                (tile_hbm, tile_ref),
                (taken_hbm, taken_ref),
                (bias_hbm, bias_ref),
                (feat_ref, comb.at[pl.ds(0, blocks)]),
                (adj_ref, adj),
                (cot_ref, cot.at[feat]),
                (ws_ref, ws.at[0]),
                (wn_ref, wn.at[0]),
                (stale_ref.at[me], back.at[0]),
            )
        )
    ]
    for load in loads[:3]:
        load.start()
    pl.semaphore_signal(barrier, inc=1, device_id=(me, 1 - feat), device_id_type=MESH)
    for dz in range(1, 8):
        pl.semaphore_signal(
            barrier,
            inc=1,
            device_id=(column_ahead(0) + z_ahead[dz], feat),
            device_id_type=MESH,
        )
    lax.fori_loop(1, PEERS // 8, greet, 0)
    for load in loads[3:]:
        load.start()
    for load in loads[1:3]:
        load.wait()

    slot_of = lax.broadcasted_iota(jnp.int32, (CAP, PEERS), 0)
    idx = jnp.where(slot_of < cnt_ref[...], idx_ref[...], -1).astype(F32)
    tiled = jnp.concatenate([idx] * GROUP, axis=0)
    lane = lax.broadcasted_iota(jnp.int32, (SLOTS, PEERS), 1)
    place = lax.broadcasted_iota(jnp.int32, (GROUP, CAP, PEERS), 0).reshape(SLOTS, PEERS)
    node = lax.broadcasted_iota(jnp.int32, (SLOTS, nodes), 1)
    loads[0].wait()

    def gather(g, carry):
        i = g * GROUP + place
        dz, dx, dy = i & 7, (i >> 3) & 3, i >> 5
        z, x, y = me & 7, (me >> 3) & 3, me >> 5
        dest = (((y + dy) & 3) * 4 + ((x + dx) & 3)) * 8 + ((z + dz) & 7)
        column = jnp.sum(jnp.where(lane == dest, tiled, 0.0), axis=1, keepdims=True)
        pick = (node == column.astype(jnp.int32)).astype(F32).astype(BF16)
        sent = jnp.dot(pick, prev[...], preferred_element_type=F32)
        out_buf[pl.ds(g * GROUP, GROUP)] = sent.reshape(GROUP, CAP, -1).astype(BF16)
        rows_of[g] = jnp.transpose(jnp.broadcast_to(column, (SLOTS, PEERS)))[:8]

        @pl.when(g == 0)
        def _():
            pl.semaphore_wait(barrier, PEERS)

        def send(base, i, dz):
            pltpu.make_async_remote_copy(
                src_ref=out_buf.at[i],
                dst_ref=recv.at[me],
                send_sem=send_sem.at[0],
                recv_sem=recv_sem,
                device_id=(base + z_ahead[dz], feat),
                device_id_type=MESH,
            ).start()

        for half in range(2):
            base = column_ahead(2 * g + half)
            if half == 0:
                pl.when(g > 0)(lambda: send(base, g * GROUP, 0))
            for dz in range(1 - half, 8):
                send(base, g * GROUP + half * 8 + dz, dz)
        return carry

    lax.fori_loop(0, GROUPS, gather, 0)
    recv[me] = out_buf[0]

    def to_pair(n, src, dst):
        return pltpu.make_async_remote_copy(
            src_ref=src,
            dst_ref=dst,
            send_sem=pair_send.at[n],
            recv_sem=pair_recv.at[n],
            device_id=(me, 1 - feat),
            device_id_type=MESH,
        )

    for load in loads[3:6]:
        load.wait()
    bias[feat] = jnp.broadcast_to(bias_ref[...], bias.shape[1:])
    pairs = [
        to_pair(CHUNKS, ws_ref, ws.at[1]),
        to_pair(CHUNKS + 1, wn_ref, wn.at[1]),
        to_pair(CHUNKS + 2, bias.at[feat], bias.at[feat]),
        to_pair(CHUNKS + 3, feat_ref, feat2),
        to_pair(CHUNKS + 4, cot_ref, cot.at[feat]),
    ]
    for pair in pairs:
        pair.start()

    def send_back(c, first):
        base = column_behind(c)
        for dz in range(first, 8):
            peer = base + z_behind[dz]
            pltpu.make_async_remote_copy(
                src_ref=stale_ref.at[peer],
                dst_ref=back.at[c * 8 + dz],
                send_sem=send_sem.at[1],
                recv_sem=back_sem.at[c // 2],
                device_id=(peer, feat),
                device_id_type=MESH,
            ).start()

    def send_back_column(c, carry):
        send_back(c, 0)
        return carry

    send_back(0, 1)
    lax.fori_loop(1, PEERS // 8, send_back_column, 0)

    sub = lax.broadcasted_iota(jnp.int32, (BLOCK, BLOCK), 0)
    lanes = lax.broadcasted_iota(jnp.int32, (BLOCK, BLOCK), 1)
    tiles = adj.shape[0]

    def spread_cols(t, carry):
        down, across = carry
        col = tile_ref[t]
        return jnp.where(sub == t, col, down), jnp.where(lanes == t, col, across)

    def count(hits, axis=0):
        return jnp.sum(jnp.where(hits, 1, 0), axis=axis, keepdims=True)

    far = jnp.full((BLOCK, BLOCK), 1000, jnp.int32)
    down, across = lax.fori_loop(0, tiles, spread_cols, (far, far))
    rank = count(across * BLOCK + lanes < down * BLOCK + sub, axis=1)
    at_rank = jnp.where(lanes == rank, 1, 0)
    follows = jnp.where(lanes == rank + 1, 1, 0)
    col_here = jnp.sum(down * at_rank, axis=0, keepdims=True)
    col_before = jnp.sum((down + 1) * follows, axis=0, keepdims=True)
    meta_v[...] = jnp.zeros(meta_v.shape, jnp.int32)
    meta_v[0:1, :] = jnp.sum(sub * at_rank, axis=0, keepdims=True)
    meta_v[1:2, :] = jnp.where(col_here + 1 == col_before, 1, 0)
    meta_v[2:3, :] = jnp.maximum(count(down <= lanes) - 1, 0)
    meta_v[3:4, :] = jnp.minimum(count(down == lanes), 1)
    meta_copy = pltpu.make_async_copy(meta_v, meta_s, out_sem.at[3])
    meta_copy.start()
    meta_copy.wait()

    all_but_one = pl.ds(0, PEERS - 1)
    for load in loads[6:]:
        load.wait()
    pltpu.make_async_copy(recv.at[all_but_one], recv.at[all_but_one], recv_sem).wait()

    def place_rows(g, carry):
        rows = recv[pl.ds(g * GROUP, GROUP)].astype(F32).reshape(SLOTS, -1).astype(BF16)
        comb[pl.ds(blocks + g * GROUP_BLOCKS, GROUP_BLOCKS)] = rows.reshape(GROUP_BLOCKS, BLOCK, -1)
        return carry

    lax.fori_loop(0, GROUPS, place_rows, 0)

    def rows_of_chunk(q):
        return pl.ds(pl.multiple_of(q * chunk, chunk), chunk)

    def agg_pair(q):
        return to_pair(q, agg.at[rows_of_chunk(q)], agg2.at[rows_of_chunk(q)])

    def aggregate(q, carry):
        def row_block(r, carry):
            left = jnp.concatenate([adj[r * TPR + j] for j in range(TPR)], axis=1)
            right = jnp.concatenate(
                [comb[tile_ref[r * TPR + j]] for j in range(TPR)], axis=0
            )
            summed = jnp.dot(left, right, preferred_element_type=F32)
            agg[pl.ds(pl.multiple_of(r * BLOCK, BLOCK), BLOCK)] = summed.astype(BF16)
            return carry

        per_chunk = chunk // BLOCK
        lax.fori_loop(q * per_chunk, (q + 1) * per_chunk, row_block, 0)
        agg_pair(q).start()
        return carry

    lax.fori_loop(0, CHUNKS, aggregate, 0)
    for pair in pairs:
        pair.wait()

    def dense(q, carry):
        agg_pair(q).wait()
        rows = rows_of_chunk(q)
        own = comb[pl.ds(q * (chunk // BLOCK), chunk // BLOCK)].reshape(chunk, -1)
        other = feat2[pl.ds(q * (chunk // BLOCK), chunk // BLOCK)].reshape(chunk, -1)
        neigh_grad = self_grad = None
        for j in range(2):
            cols = slice(j * 256, (j + 1) * 256)
            preact = jnp.dot(own, ws[0, :, cols], preferred_element_type=F32)
            preact += jnp.dot(other, ws[1, :, cols], preferred_element_type=F32)
            preact += jnp.dot(agg[rows, :], wn[0, :, cols], preferred_element_type=F32)
            preact += jnp.dot(agg2[rows, :], wn[1, :, cols], preferred_element_type=F32)
            preact += bias[j][0:1, :]
            pre_grad = jnp.where(preact > 0, cot[j, rows, :].astype(F32), 0.0).astype(BF16)
            cot[j, rows, :] = jnp.maximum(preact, 0.0).astype(BF16)
            part = lax.dot_general(
                pre_grad, wn[0, :, cols], CONTRACT_LAST, preferred_element_type=F32
            )
            neigh_grad = part if j == 0 else neigh_grad + part
            part = lax.dot_general(
                pre_grad, ws[0, :, cols], CONTRACT_LAST, preferred_element_type=F32
            )
            self_grad = part if j == 0 else self_grad + part
        agg_grad[rows, :] = neigh_grad.astype(BF16)
        total[rows, :] = self_grad
        return carry

    lax.fori_loop(0, CHUNKS, dense, 0)
    hid_copy = pltpu.make_async_copy(cot.at[feat], hid_ref, out_sem.at[0])
    hid_copy.start()

    def tile_terms(r, carry):
        left = jnp.concatenate([adj[r * TPR + j] for j in range(TPR)], axis=1)
        right = agg_grad[pl.ds(pl.multiple_of(r * BLOCK, BLOCK), BLOCK), :]
        part = lax.dot_general(left, right, CONTRACT_FIRST, preferred_element_type=F32)
        terms[pl.ds(r * TPR, TPR)] = part.reshape(TPR, BLOCK, -1)
        return carry

    lax.fori_loop(0, blocks, tile_terms, 0)

    def running(i, carry):
        carry = carry * meta_s[1, i].astype(F32) + terms[meta_s[0, i]]
        sums[i] = carry
        return carry

    lax.fori_loop(0, tiles, running, jnp.zeros(terms.shape[1:], F32))

    def column_sum(c):
        return sums[meta_s[2, c]] * meta_s[3, c].astype(F32)

    def add_local(c, carry):
        rows = pl.ds(pl.multiple_of(c * BLOCK, BLOCK), BLOCK)
        total[rows, :] += column_sum(c)
        return carry

    lax.fori_loop(0, blocks, add_local, 0)

    pltpu.make_async_copy(out_buf.at[all_but_one], out_buf.at[all_but_one], send_sem.at[0]).wait()
    slot = lax.broadcasted_iota(jnp.int32, (GROUP, CAP, 256), 1).reshape(SLOTS, 256).astype(F32)
    taken = jnp.broadcast_to(taken_ref[...].astype(F32), (SLOTS, PEERS))

    def boundary(g, carry):
        first = blocks + g * GROUP_BLOCKS
        rows = jnp.concatenate([column_sum(first + n) for n in range(GROUP_BLOCKS)], axis=0)
        limit = jnp.sum(
            jnp.where(lane == g * GROUP + place, taken, 0.0), axis=1, keepdims=True
        )
        rows = jnp.where(slot < limit, rows, 0.0)
        out_buf[pl.ds(g * GROUP, GROUP)] = rows.reshape(GROUP, CAP, -1).astype(BF16)
        return carry

    lax.fori_loop(0, GROUPS, boundary, 0)
    bnd_copy = pltpu.make_async_copy(out_buf, bnd_ref, out_sem.at[1])
    bnd_copy.start()

    def out_piece(p):
        rows = pl.ds(pl.multiple_of(p * PIECE, PIECE), PIECE)
        return pltpu.make_async_copy(prev.at[rows], grad_ref.at[rows], out_sem.at[2])

    def scatter(g, first, last):
        row = rows_of[g][0:1, :]

        def mark(p, carry):
            at = lax.broadcasted_iota(jnp.int32, (PIECE, SLOTS), 0) + p * PIECE
            hit = jnp.where(at.astype(F32) == row, 1.0, 0.0)
            spread[pl.ds(pl.multiple_of(p * PIECE, PIECE), PIECE), :] = hit.astype(BF16)
            return carry

        lax.fori_loop(0, nodes // PIECE, mark, 0)
        arrived = back.at[pl.ds(0, GROUP - first)]
        pltpu.make_async_copy(arrived, arrived, back_sem.at[g]).wait()
        values = back[pl.ds(g * GROUP, GROUP)].astype(F32).reshape(SLOTS, -1).astype(BF16)

        def add(p, carry):
            rows = pl.ds(pl.multiple_of(p * PIECE, PIECE), PIECE)
            added = total[rows, :] + jnp.dot(spread[rows, :], values, preferred_element_type=F32)
            if last:
                prev[rows, :] = added.astype(BF16)
                out_piece(p).start()
            else:
                total[rows, :] = added
            return carry

        lax.fori_loop(0, nodes // PIECE, add, 0)

    scatter(0, 1, False)

    def scatter_group(g, carry):
        scatter(g, 0, False)
        return carry

    lax.fori_loop(1, GROUPS - 1, scatter_group, 0)
    scatter(GROUPS - 1, 0, True)
    pltpu.make_async_copy(back.at[all_but_one], back.at[all_but_one], send_sem.at[1]).wait()
    hid_copy.wait()
    bnd_copy.wait()
    pltpu.make_async_copy(prev, grad_ref, out_sem.at[2]).wait()


def hand_over(
    hid_in, grad_in, bnd_in, hid_out, grad_out, bnd_out, hid, grad, bnd, load_sem, store_sem
):
    loads, stores = [], []
    triples = ((hid_in, hid, hid_out), (grad_in, grad, grad_out), (bnd_in, bnd, bnd_out))
    for n, (src, held, dst) in enumerate(triples):
        step = held.shape[0] // PARTS
        for part in range(PARTS):
            piece = pl.ds(part * step, step)
            loads.append(
                pltpu.make_async_copy(src.at[piece], held.at[piece], load_sem.at[n, part])
            )
            stores.append(
                pltpu.make_async_copy(held.at[piece], dst.at[piece], store_sem.at[n, part])
            )
    for load in loads:
        load.start()
    for load, store in zip(loads, stores):
        load.wait()
        store.start()
    for store in stores:
        store.wait()


def per_device(
    features,
    prev_features,
    cotangent,
    adjacency,
    tile_cols,
    send_idx,
    send_cnt,
    recv_cnt,
    stale_grad,
    w_self,
    w_neigh,
    layer_bias,
):
    nodes, width = features.shape
    tiles = adjacency.shape[0]
    rows = jax.ShapeDtypeStruct((nodes, width), BF16)
    slots = jax.ShapeDtypeStruct((PEERS, CAP, width), BF16)
    anywhere = pl.BlockSpec(memory_space=pl.ANY)
    dma = pltpu.SemaphoreType.DMA
    whole = pltpu.VMEM((nodes, width), BF16)
    results = pl.pallas_call(
        layer_kernel,
        out_shape=[rows, rows, slots],
        in_specs=[anywhere] * 12,
        out_specs=[anywhere] * 3,
        scratch_shapes=[
            pltpu.SMEM(tile_cols.shape, jnp.int32),
            pltpu.VMEM((CAP, PEERS), jnp.int32),
            pltpu.VMEM((1, PEERS), jnp.int32),
            pltpu.VMEM((1, PEERS), jnp.int32),
            pltpu.VMEM((1, width), F32),
            whole,
            pltpu.VMEM((nodes // BLOCK + GROUPS * GROUP_BLOCKS, BLOCK, width), BF16),
            pltpu.VMEM((nodes // BLOCK, BLOCK, width), BF16),
            pltpu.VMEM((2, nodes, width), BF16),
            pltpu.VMEM((2,) + w_self.shape, BF16),
            pltpu.VMEM((2,) + w_neigh.shape, BF16),
            pltpu.VMEM((2, 8, width), F32),
            pltpu.VMEM(adjacency.shape, BF16),
            pltpu.VMEM((PEERS, CAP, width), BF16),
            pltpu.VMEM((PEERS, CAP, width), BF16),
            pltpu.VMEM((PEERS, CAP, width), BF16),
            whole,
            whole,
            whole,
            pltpu.VMEM((nodes, width), F32),
            pltpu.VMEM((tiles, BLOCK, width), F32),
            pltpu.VMEM((tiles, BLOCK, width), F32),
            pltpu.VMEM((nodes, SLOTS), BF16),
            pltpu.VMEM((GROUPS, 8, SLOTS), F32),
            pltpu.VMEM((8, BLOCK), jnp.int32),
            pltpu.SMEM((8, BLOCK), jnp.int32),
            dma((12,)),
            dma((2,)),
            dma,
            dma((GROUPS,)),
            dma((CHUNKS + 5,)),
            dma((CHUNKS + 5,)),
            dma((4,)),
        ],
        compiler_params=pltpu.CompilerParams(
            collective_id=0, has_side_effects=True, vmem_limit_bytes=62 << 20
        ),
    )(
        tile_cols,
        send_idx.T,
        send_cnt.reshape(1, PEERS),
        recv_cnt.reshape(1, PEERS),
        layer_bias.reshape(1, width),
        features.reshape(nodes // BLOCK, BLOCK, width),
        prev_features,
        cotangent,
        adjacency,
        stale_grad,
        w_self,
        w_neigh,
    )
    return pl.pallas_call(
        hand_over,
        out_shape=[rows, rows, slots],
        in_specs=[anywhere] * 3,
        out_specs=[anywhere] * 3,
        scratch_shapes=[
            whole,
            whole,
            pltpu.VMEM((PEERS, CAP, width), BF16),
            dma((3, PARTS)),
            dma((3, PARTS)),
        ],
        compiler_params=pltpu.CompilerParams(vmem_limit_bytes=62 << 20),
    )(*results)


def solution(mesh):
    return jax.shard_map(
        per_device,
        mesh=mesh,
        in_specs=(
            P("dom", "feat"),
            P("dom", "feat"),
            P("dom", "feat"),
            P("dom", None, None),
            P("dom"),
            P("dom", None),
            P("dom"),
            P("dom"),
            P("dom", None, "feat"),
            P("feat", None),
            P("feat", None),
            P("feat"),
        ),
        out_specs=(P("dom", "feat"), P("dom", "feat"), P("dom", None, "feat")),
        check_vma=False,
    )
```

```python
import jax
import jax.numpy as jnp
from jax import lax
from jax.experimental import pallas as pl
from jax.experimental.pallas import tpu as pltpu
from jax.sharding import PartitionSpec as P

MESH = pl.DeviceIdType.MESH
BF16, F32 = jnp.bfloat16, jnp.float32
PEERS = 128
CAP = 24
GROUP = 16
GROUPS = PEERS // GROUP
SLOTS = GROUP * CAP
BLOCK = 128
GROUP_BLOCKS = SLOTS // BLOCK
TPR = 6
CHUNKS = 4
FINISH_MB = 6
PIECE = 256
HOPS = [[min(c // 4, 4 - c // 4) + min(c % 4, 4 - c % 4) + min(z, 8 - z) for z in range(8)] for c in range(16)]
FAR_FIRST = sorted(
    ((c, dz) for c in range(16) for dz in range(8) if c or dz), key=lambda at: -HOPS[at[0]][at[1]]
)
CONTRACT_LAST = (((1,), (1,)), ((), ()))
CONTRACT_FIRST = (((0,), (0,)), ((), ()))


def torus(me, sign):
    z, x, y = lax.rem(me, 8), lax.rem(me // 8, 4), me // 32

    def column(c):
        dy, dx = c // 4, lax.rem(c, 4)
        if sign < 0:
            dy, dx = 4 - dy, 4 - dx
        return (lax.rem(y + dy, 4) * 4 + lax.rem(x + dx, 4)) * 8

    return column, [lax.rem(z + 8 + sign * dz, 8) for dz in range(8)]


def layer_kernel(
    tile_hbm,
    idx_hbm,
    cnt_hbm,
    taken_hbm,
    bias_hbm,
    feat_ref,
    prev_ref,
    cot_ref,
    adj_ref,
    stale_ref,
    ws_ref,
    wn_ref,
    hid_ref,
    bnd_ref,
    total_ref,
    spread_ref,
    last_ref,
    tile_ref,
    idx_ref,
    cnt_ref,
    taken_ref,
    bias_ref,
    prev,
    comb,
    feat2,
    cot,
    ws,
    wn,
    bias,
    adj,
    out_buf,
    recv,
    back,
    agg,
    agg2,
    agg_grad,
    total,
    terms,
    sums,
    spread,
    rows_of,
    meta_v,
    meta_s,
    load_sem,
    send_sem,
    recv_sem,
    back_sem,
    pair_send,
    pair_recv,
    out_sem,
):
    me, feat = lax.axis_index("dom"), lax.axis_index("feat")
    nodes = prev.shape[0]
    chunk = nodes // CHUNKS
    blocks = nodes // BLOCK
    barrier = pltpu.get_barrier_semaphore()

    column_ahead, z_ahead = torus(me, 1)
    column_behind, z_behind = torus(me, -1)

    loads = [
        pltpu.make_async_copy(src, dst, load_sem.at[n])
        for n, (src, dst) in enumerate(
            (
                (prev_ref, prev),
                (idx_hbm, idx_ref),
                (cnt_hbm, cnt_ref),
                (tile_hbm, tile_ref),
                (taken_hbm, taken_ref),
                (bias_hbm, bias_ref),
                (feat_ref, comb.at[pl.ds(0, blocks)]),
                (adj_ref, adj),
                (cot_ref, cot.at[feat]),
                (ws_ref, ws.at[0]),
                (wn_ref, wn.at[0]),
                (stale_ref.at[me], back.at[0]),
            )
        )
    ]
    for load in loads[:3]:
        load.start()
    pl.semaphore_signal(barrier, inc=1, device_id=(me, 1 - feat), device_id_type=MESH)
    columns = [column_ahead(c) for c in range(PEERS // 8)]
    for c, dz in FAR_FIRST:
        peer = columns[c] + z_ahead[dz]
        pl.semaphore_signal(barrier, inc=1, device_id=(peer, feat), device_id_type=MESH)
    for load in loads[3:]:
        load.start()
    for load in loads[1:3]:
        load.wait()

    slot_of = lax.broadcasted_iota(jnp.int32, (CAP, PEERS), 0)
    idx = jnp.where(slot_of < cnt_ref[...], idx_ref[...], -1).astype(F32)
    tiled = jnp.concatenate([idx] * GROUP, axis=0)
    lane = lax.broadcasted_iota(jnp.int32, (SLOTS, PEERS), 1)
    place = lax.broadcasted_iota(jnp.int32, (GROUP, CAP, PEERS), 0).reshape(SLOTS, PEERS)
    node = lax.broadcasted_iota(jnp.int32, (SLOTS, nodes), 1)
    loads[0].wait()

    def gather(g, carry):
        i = g * GROUP + place
        dz, dx, dy = i & 7, (i >> 3) & 3, i >> 5
        z, x, y = me & 7, (me >> 3) & 3, me >> 5
        dest = (((y + dy) & 3) * 4 + ((x + dx) & 3)) * 8 + ((z + dz) & 7)
        column = jnp.sum(jnp.where(lane == dest, tiled, 0.0), axis=1, keepdims=True)
        pick = (node == column.astype(jnp.int32)).astype(F32).astype(BF16)
        sent = jnp.dot(pick, prev[...], preferred_element_type=F32)
        out_buf[pl.ds(g * GROUP, GROUP)] = sent.reshape(GROUP, CAP, -1).astype(BF16)
        rows_of[g] = jnp.transpose(jnp.broadcast_to(column, (SLOTS, PEERS)))[:8]

        @pl.when(g == 0)
        def _():
            pl.semaphore_wait(barrier, PEERS)

        def send(base, i, dz):
            pltpu.make_async_remote_copy(
                src_ref=out_buf.at[i],
                dst_ref=recv.at[me],
                send_sem=send_sem.at[0],
                recv_sem=recv_sem,
                device_id=(base + z_ahead[dz], feat),
                device_id_type=MESH,
            ).start()

        for half in range(2):
            base = column_ahead(2 * g + half)
            if half == 0:
                pl.when(g > 0)(lambda: send(base, g * GROUP, 0))
            for dz in range(1 - half, 8):
                send(base, g * GROUP + half * 8 + dz, dz)
        return carry

    lax.fori_loop(0, GROUPS, gather, 0)
    recv[me] = out_buf[0]

    def to_pair(n, src, dst):
        return pltpu.make_async_remote_copy(
            src_ref=src,
            dst_ref=dst,
            send_sem=pair_send.at[n],
            recv_sem=pair_recv.at[n],
            device_id=(me, 1 - feat),
            device_id_type=MESH,
        )

    for load in loads[3:6]:
        load.wait()
    bias[feat] = jnp.broadcast_to(bias_ref[...], bias.shape[1:])
    pairs = [
        to_pair(CHUNKS, ws_ref, ws.at[1]),
        to_pair(CHUNKS + 1, wn_ref, wn.at[1]),
        to_pair(CHUNKS + 2, bias.at[feat], bias.at[feat]),
        to_pair(CHUNKS + 3, feat_ref, feat2),
        to_pair(CHUNKS + 4, cot_ref, cot.at[feat]),
    ]
    for pair in pairs:
        pair.start()

    def send_back(c, first, into=None, base_slot=0):
        base = column_behind(c)
        for dz in range(first, 8):
            peer = base + z_behind[dz]
            pltpu.make_async_remote_copy(
                src_ref=stale_ref.at[peer],
                dst_ref=(back if into is None else into).at[c * 8 + dz - base_slot],
                send_sem=send_sem.at[1],
                recv_sem=back_sem.at[c // 2],
                device_id=(peer, feat),
                device_id_type=MESH,
            ).start()

    def send_back_column(c, carry):
        send_back(c, 0)
        return carry

    send_back(0, 1)
    lax.fori_loop(1, PEERS // 8 - 2, send_back_column, 0)
    for c in (PEERS // 8 - 2, PEERS // 8 - 1):
        send_back(c, 0, last_ref, PEERS - GROUP)

    sub = lax.broadcasted_iota(jnp.int32, (BLOCK, BLOCK), 0)
    lanes = lax.broadcasted_iota(jnp.int32, (BLOCK, BLOCK), 1)
    tiles = adj.shape[0]

    def spread_cols(t, carry):
        down, across = carry
        col = tile_ref[t]
        return jnp.where(sub == t, col, down), jnp.where(lanes == t, col, across)

    def count(hits, axis=0):
        return jnp.sum(jnp.where(hits, 1, 0), axis=axis, keepdims=True)

    far = jnp.full((BLOCK, BLOCK), 1000, jnp.int32)
    down, across = lax.fori_loop(0, tiles, spread_cols, (far, far))
    rank = count(across * BLOCK + lanes < down * BLOCK + sub, axis=1)
    at_rank = jnp.where(lanes == rank, 1, 0)
    follows = jnp.where(lanes == rank + 1, 1, 0)
    col_here = jnp.sum(down * at_rank, axis=0, keepdims=True)
    col_before = jnp.sum((down + 1) * follows, axis=0, keepdims=True)
    meta_v[...] = jnp.zeros(meta_v.shape, jnp.int32)
    meta_v[0:1, :] = jnp.sum(sub * at_rank, axis=0, keepdims=True)
    meta_v[1:2, :] = jnp.where(col_here + 1 == col_before, 1, 0)
    meta_v[2:3, :] = jnp.maximum(count(down <= lanes) - 1, 0)
    meta_v[3:4, :] = jnp.minimum(count(down == lanes), 1)
    meta_copy = pltpu.make_async_copy(meta_v, meta_s, out_sem.at[4])
    meta_copy.start()
    meta_copy.wait()

    all_but_one = pl.ds(0, PEERS - 1)
    for load in loads[6:]:
        load.wait()
    pltpu.make_async_copy(recv.at[all_but_one], recv.at[all_but_one], recv_sem).wait()

    def place_rows(g, carry):
        rows = recv[pl.ds(g * GROUP, GROUP)].astype(F32).reshape(SLOTS, -1).astype(BF16)
        comb[pl.ds(blocks + g * GROUP_BLOCKS, GROUP_BLOCKS)] = rows.reshape(GROUP_BLOCKS, BLOCK, -1)
        return carry

    lax.fori_loop(0, GROUPS, place_rows, 0)

    def rows_of_chunk(q):
        return pl.ds(pl.multiple_of(q * chunk, chunk), chunk)

    def agg_pair(q):
        return to_pair(q, agg.at[rows_of_chunk(q)], agg2.at[rows_of_chunk(q)])

    def aggregate(q, carry):
        def row_block(r, carry):
            left = jnp.concatenate([adj[r * TPR + j] for j in range(TPR)], axis=1)
            right = jnp.concatenate(
                [comb[tile_ref[r * TPR + j]] for j in range(TPR)], axis=0
            )
            summed = jnp.dot(left, right, preferred_element_type=F32)
            agg[pl.ds(pl.multiple_of(r * BLOCK, BLOCK), BLOCK)] = summed.astype(BF16)
            return carry

        per_chunk = chunk // BLOCK
        lax.fori_loop(q * per_chunk, (q + 1) * per_chunk, row_block, 0)
        agg_pair(q).start()
        return carry

    lax.fori_loop(0, CHUNKS, aggregate, 0)
    for pair in pairs:
        pair.wait()

    def dense(q, carry):
        agg_pair(q).wait()
        rows = rows_of_chunk(q)
        own = comb[pl.ds(q * (chunk // BLOCK), chunk // BLOCK)].reshape(chunk, -1)
        other = feat2[pl.ds(q * (chunk // BLOCK), chunk // BLOCK)].reshape(chunk, -1)
        neigh_grad = self_grad = None
        for j in range(2):
            cols = slice(j * 256, (j + 1) * 256)
            preact = jnp.dot(own, ws[0, :, cols], preferred_element_type=F32)
            preact += jnp.dot(other, ws[1, :, cols], preferred_element_type=F32)
            preact += jnp.dot(agg[rows, :], wn[0, :, cols], preferred_element_type=F32)
            preact += jnp.dot(agg2[rows, :], wn[1, :, cols], preferred_element_type=F32)
            preact += bias[j][0:1, :]
            pre_grad = jnp.where(preact > 0, cot[j, rows, :].astype(F32), 0.0).astype(BF16)
            cot[j, rows, :] = jnp.maximum(preact, 0.0).astype(BF16)
            part = lax.dot_general(
                pre_grad, wn[0, :, cols], CONTRACT_LAST, preferred_element_type=F32
            )
            neigh_grad = part if j == 0 else neigh_grad + part
            part = lax.dot_general(
                pre_grad, ws[0, :, cols], CONTRACT_LAST, preferred_element_type=F32
            )
            self_grad = part if j == 0 else self_grad + part
        agg_grad[rows, :] = neigh_grad.astype(BF16)
        total[rows, :] = self_grad
        return carry

    lax.fori_loop(0, CHUNKS, dense, 0)
    hid_copy = pltpu.make_async_copy(cot.at[feat], hid_ref, out_sem.at[0])
    hid_copy.start()

    def tile_terms(r, carry):
        left = jnp.concatenate([adj[r * TPR + j] for j in range(TPR)], axis=1)
        right = agg_grad[pl.ds(pl.multiple_of(r * BLOCK, BLOCK), BLOCK), :]
        part = lax.dot_general(left, right, CONTRACT_FIRST, preferred_element_type=F32)
        terms[pl.ds(r * TPR, TPR)] = part.reshape(TPR, BLOCK, -1)
        return carry

    lax.fori_loop(0, blocks, tile_terms, 0)

    def running(i, carry):
        carry = carry * meta_s[1, i].astype(F32) + terms[meta_s[0, i]]
        sums[i] = carry
        return carry

    lax.fori_loop(0, tiles, running, jnp.zeros(terms.shape[1:], F32))

    def column_sum(c):
        return sums[meta_s[2, c]] * meta_s[3, c].astype(F32)

    def add_local(c, carry):
        rows = pl.ds(pl.multiple_of(c * BLOCK, BLOCK), BLOCK)
        total[rows, :] += column_sum(c)
        return carry

    lax.fori_loop(0, blocks, add_local, 0)

    pltpu.make_async_copy(out_buf.at[all_but_one], out_buf.at[all_but_one], send_sem.at[0]).wait()
    slot = lax.broadcasted_iota(jnp.int32, (GROUP, CAP, 256), 1).reshape(SLOTS, 256).astype(F32)
    taken = jnp.broadcast_to(taken_ref[...].astype(F32), (SLOTS, PEERS))

    def boundary(g, carry):
        first = blocks + g * GROUP_BLOCKS
        rows = jnp.concatenate([column_sum(first + n) for n in range(GROUP_BLOCKS)], axis=0)
        limit = jnp.sum(
            jnp.where(lane == g * GROUP + place, taken, 0.0), axis=1, keepdims=True
        )
        rows = jnp.where(slot < limit, rows, 0.0)
        out_buf[pl.ds(g * GROUP, GROUP)] = rows.reshape(GROUP, CAP, -1).astype(BF16)
        return carry

    lax.fori_loop(0, GROUPS, boundary, 0)
    bnd_copy = pltpu.make_async_copy(out_buf, bnd_ref, out_sem.at[1])
    bnd_copy.start()

    def mark_group(g):
        row = rows_of[g][0:1, :]

        def mark(p, carry):
            at = lax.broadcasted_iota(jnp.int32, (PIECE, SLOTS), 0) + p * PIECE
            hit = jnp.where(at.astype(F32) == row, 1.0, 0.0)
            spread[pl.ds(pl.multiple_of(p * PIECE, PIECE), PIECE), :] = hit.astype(BF16)
            return carry

        lax.fori_loop(0, nodes // PIECE, mark, 0)

    def scatter(g, first):
        mark_group(g)
        arrived = back.at[pl.ds(0, GROUP - first)]
        pltpu.make_async_copy(arrived, arrived, back_sem.at[g]).wait()
        values = back[pl.ds(g * GROUP, GROUP)].astype(F32).reshape(SLOTS, -1).astype(BF16)

        def add(p, carry):
            rows = pl.ds(pl.multiple_of(p * PIECE, PIECE), PIECE)
            total[rows, :] += jnp.dot(spread[rows, :], values, preferred_element_type=F32)
            return carry

        lax.fori_loop(0, nodes // PIECE, add, 0)

    scatter(0, 1)

    def scatter_group(g, carry):
        scatter(g, 0)
        return carry

    lax.fori_loop(1, GROUPS - 1, scatter_group, 0)

    total_copy = pltpu.make_async_copy(total, total_ref, out_sem.at[2])
    total_copy.start()
    mark_group(GROUPS - 1)
    spread_copy = pltpu.make_async_copy(spread, spread_ref, out_sem.at[3])
    spread_copy.start()
    pltpu.make_async_copy(last_ref, last_ref, back_sem.at[GROUPS - 1]).wait()
    pltpu.make_async_copy(recv.at[all_but_one], recv.at[all_but_one], send_sem.at[1]).wait()
    for copy in (hid_copy, bnd_copy, total_copy, spread_copy):
        copy.wait()


def finish_kernel(hid, bnd, total, spread, last, hid_out, grad_out, bnd_out, grad, sem):
    whole = [
        pltpu.make_async_copy(hid, hid_out, sem.at[0]),
        pltpu.make_async_copy(bnd, bnd_out, sem.at[1]),
    ]
    for copy in whole:
        copy.start()
    values = last[...].astype(F32).reshape(SLOTS, -1).astype(BF16)
    for p in range(grad.shape[0] // PIECE):
        rows = pl.ds(p * PIECE, PIECE)
        added = total[rows, :] + jnp.dot(spread[rows, :], values, preferred_element_type=F32)
        grad[rows, :] = added.astype(BF16)
        pltpu.make_async_copy(grad.at[rows], grad_out.at[rows], sem.at[2]).start()
    for copy in whole:
        copy.wait()
    pltpu.make_async_copy(grad, grad_out, sem.at[2]).wait()


def per_device(
    features,
    prev_features,
    cotangent,
    adjacency,
    tile_cols,
    send_idx,
    send_cnt,
    recv_cnt,
    stale_grad,
    w_self,
    w_neigh,
    layer_bias,
):
    nodes, width = features.shape
    tiles = adjacency.shape[0]
    rows = jax.ShapeDtypeStruct((nodes, width), BF16)
    slots = jax.ShapeDtypeStruct((PEERS, CAP, width), BF16)
    anywhere = pl.BlockSpec(memory_space=pl.ANY)
    vmem = pl.BlockSpec(memory_space=pltpu.VMEM)
    dma = pltpu.SemaphoreType.DMA
    whole = pltpu.VMEM((nodes, width), BF16)
    results = pl.pallas_call(
        layer_kernel,
        out_shape=[
            whole,
            pltpu.VMEM((PEERS, CAP, width), BF16),
            pltpu.VMEM((nodes, width), F32),
            pltpu.VMEM((nodes, SLOTS), BF16),
            pltpu.VMEM((GROUP, CAP, width), BF16),
        ],
        in_specs=[anywhere] * 12,
        out_specs=[anywhere] * 5,
        scratch_shapes=[
            pltpu.SMEM(tile_cols.shape, jnp.int32),
            pltpu.VMEM((CAP, PEERS), jnp.int32),
            pltpu.VMEM((1, PEERS), jnp.int32),
            pltpu.VMEM((1, PEERS), jnp.int32),
            pltpu.VMEM((1, width), F32),
            whole,
            pltpu.VMEM((nodes // BLOCK + GROUPS * GROUP_BLOCKS, BLOCK, width), BF16),
            pltpu.VMEM((nodes // BLOCK, BLOCK, width), BF16),
            pltpu.VMEM((2, nodes, width), BF16),
            pltpu.VMEM((2,) + w_self.shape, BF16),
            pltpu.VMEM((2,) + w_neigh.shape, BF16),
            pltpu.VMEM((2, 8, width), F32),
            pltpu.VMEM(adjacency.shape, BF16),
            pltpu.VMEM((PEERS, CAP, width), BF16),
            pltpu.VMEM((PEERS, CAP, width), BF16),
            pltpu.VMEM((PEERS - GROUP, CAP, width), BF16),
            whole,
            whole,
            whole,
            pltpu.VMEM((nodes, width), F32),
            pltpu.VMEM((tiles, BLOCK, width), F32),
            pltpu.VMEM((tiles, BLOCK, width), F32),
            pltpu.VMEM((nodes, SLOTS), BF16),
            pltpu.VMEM((GROUPS, 8, SLOTS), F32),
            pltpu.VMEM((8, BLOCK), jnp.int32),
            pltpu.SMEM((8, BLOCK), jnp.int32),
            dma((12,)),
            dma((2,)),
            dma,
            dma((GROUPS,)),
            dma((CHUNKS + 5,)),
            dma((CHUNKS + 5,)),
            dma((5,)),
        ],
        compiler_params=pltpu.CompilerParams(
            collective_id=0, has_side_effects=True, vmem_limit_bytes=53 << 20
        ),
    )(
        tile_cols,
        send_idx.T,
        send_cnt.reshape(1, PEERS),
        recv_cnt.reshape(1, PEERS),
        layer_bias.reshape(1, width),
        features.reshape(nodes // BLOCK, BLOCK, width),
        prev_features,
        cotangent,
        adjacency,
        stale_grad,
        w_self,
        w_neigh,
    )
    return pl.pallas_call(
        finish_kernel,
        out_shape=[rows, rows, slots],
        in_specs=[vmem] * 5,
        out_specs=[anywhere] * 3,
        scratch_shapes=[whole, dma((3,))],
        compiler_params=pltpu.CompilerParams(vmem_limit_bytes=FINISH_MB << 20),
    )(*[pltpu.with_memory_space_constraint(result, pltpu.VMEM) for result in results])


def solution(mesh):
    return jax.shard_map(
        per_device,
        mesh=mesh,
        in_specs=(
            P("dom", "feat"),
            P("dom", "feat"),
            P("dom", "feat"),
            P("dom", None, None),
            P("dom"),
            P("dom", None),
            P("dom"),
            P("dom"),
            P("dom", None, "feat"),
            P("feat", None),
            P("feat", None),
            P("feat"),
        ),
        out_specs=(P("dom", "feat"), P("dom", "feat"), P("dom", None, "feat")),
        check_vma=False,
    )
```

```python
import jax
import jax.numpy as jnp
from jax import lax
from jax.experimental import pallas as pl
from jax.experimental.pallas import tpu as pltpu
from jax.sharding import PartitionSpec as P

MESH = pl.DeviceIdType.MESH
BF16, F32 = jnp.bfloat16, jnp.float32
PEERS = 128
CAP = 24
GROUP = 16
GROUPS = PEERS // GROUP
SLOTS = GROUP * CAP
BLOCK = 128
GROUP_BLOCKS = SLOTS // BLOCK
TPR = 6
CHUNKS = 4
FINISH_MB = 6
PIECE = 256
HOPS = [[min(c // 4, 4 - c // 4) + min(c % 4, 4 - c % 4) + min(z, 8 - z) for z in range(8)] for c in range(16)]
FAR_FIRST = sorted(
    ((c, dz) for c in range(16) for dz in range(8) if c or dz), key=lambda at: -HOPS[at[0]][at[1]]
)
FAR_Z = (0, 4, 3, 5, 2, 6, 1, 7)
CONTRACT_LAST = (((1,), (1,)), ((), ()))
CONTRACT_FIRST = (((0,), (0,)), ((), ()))


def torus(me, sign):
    z, x, y = lax.rem(me, 8), lax.rem(me // 8, 4), me // 32

    def column(c):
        dy, dx = c // 4, lax.rem(c, 4)
        if sign < 0:
            dy, dx = 4 - dy, 4 - dx
        return (lax.rem(y + dy, 4) * 4 + lax.rem(x + dx, 4)) * 8

    return column, [lax.rem(z + 8 + sign * dz, 8) for dz in range(8)]


def layer_kernel(
    tile_hbm,
    idx_hbm,
    cnt_hbm,
    taken_hbm,
    bias_hbm,
    feat_ref,
    prev_ref,
    cot_ref,
    adj_ref,
    stale_ref,
    ws_ref,
    wn_ref,
    hid_ref,
    bnd_ref,
    total_ref,
    spread_ref,
    last_ref,
    tile_ref,
    idx_ref,
    cnt_ref,
    taken_ref,
    bias_ref,
    prev,
    comb,
    feat2,
    cot,
    ws,
    wn,
    bias,
    adj,
    out_buf,
    recv,
    back,
    agg,
    agg2,
    agg_grad,
    total,
    terms,
    sums,
    spread,
    rows_of,
    meta_v,
    meta_s,
    load_sem,
    send_sem,
    recv_sem,
    back_sem,
    pair_send,
    pair_recv,
    out_sem,
):
    me, feat = lax.axis_index("dom"), lax.axis_index("feat")
    nodes = prev.shape[0]
    chunk = nodes // CHUNKS
    blocks = nodes // BLOCK
    barrier = pltpu.get_barrier_semaphore()

    column_ahead, z_ahead = torus(me, 1)
    column_behind, z_behind = torus(me, -1)

    loads = [
        pltpu.make_async_copy(src, dst, load_sem.at[n])
        for n, (src, dst) in enumerate(
            (
                (prev_ref, prev),
                (idx_hbm, idx_ref),
                (cnt_hbm, cnt_ref),
                (tile_hbm, tile_ref),
                (taken_hbm, taken_ref),
                (bias_hbm, bias_ref),
                (feat_ref, comb.at[pl.ds(0, blocks)]),
                (adj_ref, adj),
                (cot_ref, cot.at[feat]),
                (ws_ref, ws.at[0]),
                (wn_ref, wn.at[0]),
                (stale_ref.at[me], last_ref.at[0]),
            )
        )
    ]
    for load in loads[:3]:
        load.start()
    pl.semaphore_signal(barrier, inc=1, device_id=(me, 1 - feat), device_id_type=MESH)
    columns = [column_ahead(c) for c in range(PEERS // 8)]
    for c, dz in FAR_FIRST:
        peer = columns[c] + z_ahead[dz]
        pl.semaphore_signal(barrier, inc=1, device_id=(peer, feat), device_id_type=MESH)
    for load in loads[3:]:
        load.start()
    for load in loads[1:3]:
        load.wait()

    slot_of = lax.broadcasted_iota(jnp.int32, (CAP, PEERS), 0)
    idx = jnp.where(slot_of < cnt_ref[...], idx_ref[...], -1).astype(F32)
    tiled = jnp.concatenate([idx] * GROUP, axis=0)
    lane = lax.broadcasted_iota(jnp.int32, (SLOTS, PEERS), 1)
    place = lax.broadcasted_iota(jnp.int32, (GROUP, CAP, PEERS), 0).reshape(SLOTS, PEERS)
    node = lax.broadcasted_iota(jnp.int32, (SLOTS, nodes), 1)
    loads[0].wait()

    def gather(g, carry):
        i = g * GROUP + place
        dz, dx, dy = i & 7, (i >> 3) & 3, i >> 5
        z, x, y = me & 7, (me >> 3) & 3, me >> 5
        dest = (((y + dy) & 3) * 4 + ((x + dx) & 3)) * 8 + ((z + dz) & 7)
        column = jnp.sum(jnp.where(lane == dest, tiled, 0.0), axis=1, keepdims=True)
        pick = (node == column.astype(jnp.int32)).astype(F32).astype(BF16)
        sent = jnp.dot(pick, prev[...], preferred_element_type=F32)
        out_buf[pl.ds(g * GROUP, GROUP)] = sent.reshape(GROUP, CAP, -1).astype(BF16)
        rows_of[g] = jnp.transpose(jnp.broadcast_to(column, (SLOTS, PEERS)))[:8]

        @pl.when(g == 0)
        def _():
            pl.semaphore_wait(barrier, PEERS)

        def send(base, i, dz):
            pltpu.make_async_remote_copy(
                src_ref=out_buf.at[i],
                dst_ref=recv.at[me],
                send_sem=send_sem.at[0],
                recv_sem=recv_sem,
                device_id=(base + z_ahead[dz], feat),
                device_id_type=MESH,
            ).start()

        for half in range(2):
            base = column_ahead(2 * g + half)
            if half == 0:
                pl.when(g > 0)(lambda: send(base, g * GROUP, 0))
            for dz in FAR_Z[1 - half :]:
                send(base, g * GROUP + half * 8 + dz, dz)
        return carry

    lax.fori_loop(0, GROUPS, gather, 0)
    recv[me] = out_buf[0]

    def to_pair(n, src, dst):
        return pltpu.make_async_remote_copy(
            src_ref=src,
            dst_ref=dst,
            send_sem=pair_send.at[n],
            recv_sem=pair_recv.at[n],
            device_id=(me, 1 - feat),
            device_id_type=MESH,
        )

    for load in loads[3:6]:
        load.wait()
    bias[feat] = jnp.broadcast_to(bias_ref[...], bias.shape[1:])
    pairs = [
        to_pair(CHUNKS, ws_ref, ws.at[1]),
        to_pair(CHUNKS + 1, wn_ref, wn.at[1]),
        to_pair(CHUNKS + 2, bias.at[feat], bias.at[feat]),
        to_pair(CHUNKS + 3, feat_ref, feat2),
        to_pair(CHUNKS + 4, cot_ref, cot.at[feat]),
    ]
    for pair in pairs:
        pair.start()

    def send_back(c, first, into, base_slot):
        base = column_behind(c)
        for dz in FAR_Z[first:]:
            peer = base + z_behind[dz]
            pltpu.make_async_remote_copy(
                src_ref=stale_ref.at[peer],
                dst_ref=into.at[c * 8 + dz - base_slot],
                send_sem=send_sem.at[1],
                recv_sem=back_sem.at[c // 2],
                device_id=(peer, feat),
                device_id_type=MESH,
            ).start()

    def send_back_column(c, carry):
        send_back(PEERS // 8 - 1 - c, 0, back, GROUP)
        return carry

    lax.fori_loop(0, PEERS // 8 - 2, send_back_column, 0)
    send_back(1, 0, last_ref, 0)
    send_back(0, 1, last_ref, 0)

    sub = lax.broadcasted_iota(jnp.int32, (BLOCK, BLOCK), 0)
    lanes = lax.broadcasted_iota(jnp.int32, (BLOCK, BLOCK), 1)
    tiles = adj.shape[0]

    def spread_cols(t, carry):
        down, across = carry
        col = tile_ref[t]
        return jnp.where(sub == t, col, down), jnp.where(lanes == t, col, across)

    def count(hits, axis=0):
        return jnp.sum(jnp.where(hits, 1, 0), axis=axis, keepdims=True)

    far = jnp.full((BLOCK, BLOCK), 1000, jnp.int32)
    down, across = lax.fori_loop(0, tiles, spread_cols, (far, far))
    rank = count(across * BLOCK + lanes < down * BLOCK + sub, axis=1)
    at_rank = jnp.where(lanes == rank, 1, 0)
    follows = jnp.where(lanes == rank + 1, 1, 0)
    col_here = jnp.sum(down * at_rank, axis=0, keepdims=True)
    col_before = jnp.sum((down + 1) * follows, axis=0, keepdims=True)
    meta_v[...] = jnp.zeros(meta_v.shape, jnp.int32)
    meta_v[0:1, :] = jnp.sum(sub * at_rank, axis=0, keepdims=True)
    meta_v[1:2, :] = jnp.where(col_here + 1 == col_before, 1, 0)
    meta_v[2:3, :] = jnp.maximum(count(down <= lanes) - 1, 0)
    meta_v[3:4, :] = jnp.minimum(count(down == lanes), 1)
    meta_copy = pltpu.make_async_copy(meta_v, meta_s, out_sem.at[4])
    meta_copy.start()
    meta_copy.wait()

    all_but_one = pl.ds(0, PEERS - 1)
    for load in loads[6:]:
        load.wait()
    pltpu.make_async_copy(recv.at[all_but_one], recv.at[all_but_one], recv_sem).wait()

    def place_rows(g, carry):
        rows = recv[pl.ds(g * GROUP, GROUP)].astype(F32).reshape(SLOTS, -1).astype(BF16)
        comb[pl.ds(blocks + g * GROUP_BLOCKS, GROUP_BLOCKS)] = rows.reshape(GROUP_BLOCKS, BLOCK, -1)
        return carry

    lax.fori_loop(0, GROUPS, place_rows, 0)

    def rows_of_chunk(q):
        return pl.ds(pl.multiple_of(q * chunk, chunk), chunk)

    def agg_pair(q):
        return to_pair(q, agg.at[rows_of_chunk(q)], agg2.at[rows_of_chunk(q)])

    def aggregate(q, carry):
        def row_block(r, carry):
            left = jnp.concatenate([adj[r * TPR + j] for j in range(TPR)], axis=1)
            right = jnp.concatenate(
                [comb[tile_ref[r * TPR + j]] for j in range(TPR)], axis=0
            )
            summed = jnp.dot(left, right, preferred_element_type=F32)
            agg[pl.ds(pl.multiple_of(r * BLOCK, BLOCK), BLOCK)] = summed.astype(BF16)
            return carry

        per_chunk = chunk // BLOCK
        lax.fori_loop(q * per_chunk, (q + 1) * per_chunk, row_block, 0)
        agg_pair(q).start()
        return carry

    lax.fori_loop(0, CHUNKS, aggregate, 0)
    for pair in pairs:
        pair.wait()

    def dense(q, carry):
        agg_pair(q).wait()
        rows = rows_of_chunk(q)
        own = comb[pl.ds(q * (chunk // BLOCK), chunk // BLOCK)].reshape(chunk, -1)
        other = feat2[pl.ds(q * (chunk // BLOCK), chunk // BLOCK)].reshape(chunk, -1)
        neigh_grad = self_grad = None
        for j in range(2):
            cols = slice(j * 256, (j + 1) * 256)
            preact = jnp.dot(own, ws[0, :, cols], preferred_element_type=F32)
            preact += jnp.dot(other, ws[1, :, cols], preferred_element_type=F32)
            preact += jnp.dot(agg[rows, :], wn[0, :, cols], preferred_element_type=F32)
            preact += jnp.dot(agg2[rows, :], wn[1, :, cols], preferred_element_type=F32)
            preact += bias[j][0:1, :]
            pre_grad = jnp.where(preact > 0, cot[j, rows, :].astype(F32), 0.0).astype(BF16)
            cot[j, rows, :] = jnp.maximum(preact, 0.0).astype(BF16)
            part = lax.dot_general(
                pre_grad, wn[0, :, cols], CONTRACT_LAST, preferred_element_type=F32
            )
            neigh_grad = part if j == 0 else neigh_grad + part
            part = lax.dot_general(
                pre_grad, ws[0, :, cols], CONTRACT_LAST, preferred_element_type=F32
            )
            self_grad = part if j == 0 else self_grad + part
        agg_grad[rows, :] = neigh_grad.astype(BF16)
        total[rows, :] = self_grad
        return carry

    lax.fori_loop(0, CHUNKS, dense, 0)
    hid_copy = pltpu.make_async_copy(cot.at[feat], hid_ref, out_sem.at[0])
    hid_copy.start()

    def tile_terms(r, carry):
        left = jnp.concatenate([adj[r * TPR + j] for j in range(TPR)], axis=1)
        right = agg_grad[pl.ds(pl.multiple_of(r * BLOCK, BLOCK), BLOCK), :]
        part = lax.dot_general(left, right, CONTRACT_FIRST, preferred_element_type=F32)
        terms[pl.ds(r * TPR, TPR)] = part.reshape(TPR, BLOCK, -1)
        return carry

    lax.fori_loop(0, blocks, tile_terms, 0)

    def running(i, carry):
        carry = carry * meta_s[1, i].astype(F32) + terms[meta_s[0, i]]
        sums[i] = carry
        return carry

    lax.fori_loop(0, tiles, running, jnp.zeros(terms.shape[1:], F32))

    def column_sum(c):
        return sums[meta_s[2, c]] * meta_s[3, c].astype(F32)

    def add_local(c, carry):
        rows = pl.ds(pl.multiple_of(c * BLOCK, BLOCK), BLOCK)
        total[rows, :] += column_sum(c)
        return carry

    lax.fori_loop(0, blocks, add_local, 0)

    pltpu.make_async_copy(out_buf.at[all_but_one], out_buf.at[all_but_one], send_sem.at[0]).wait()
    slot = lax.broadcasted_iota(jnp.int32, (GROUP, CAP, 256), 1).reshape(SLOTS, 256).astype(F32)
    taken = jnp.broadcast_to(taken_ref[...].astype(F32), (SLOTS, PEERS))

    def boundary(g, carry):
        first = blocks + g * GROUP_BLOCKS
        rows = jnp.concatenate([column_sum(first + n) for n in range(GROUP_BLOCKS)], axis=0)
        limit = jnp.sum(
            jnp.where(lane == g * GROUP + place, taken, 0.0), axis=1, keepdims=True
        )
        rows = jnp.where(slot < limit, rows, 0.0)
        out_buf[pl.ds(g * GROUP, GROUP)] = rows.reshape(GROUP, CAP, -1).astype(BF16)
        return carry

    lax.fori_loop(0, GROUPS, boundary, 0)
    bnd_copy = pltpu.make_async_copy(out_buf, bnd_ref, out_sem.at[1])
    bnd_copy.start()

    def mark_group(g):
        row = rows_of[g][0:1, :]

        def mark(p, carry):
            at = lax.broadcasted_iota(jnp.int32, (PIECE, SLOTS), 0) + p * PIECE
            hit = jnp.where(at.astype(F32) == row, 1.0, 0.0)
            spread[pl.ds(pl.multiple_of(p * PIECE, PIECE), PIECE), :] = hit.astype(BF16)
            return carry

        lax.fori_loop(0, nodes // PIECE, mark, 0)

    def scatter(n, carry):
        g = GROUPS - 1 - n
        mark_group(g)
        arrived = back.at[pl.ds(0, GROUP)]
        pltpu.make_async_copy(arrived, arrived, back_sem.at[g]).wait()
        values = back[pl.ds((g - 1) * GROUP, GROUP)].astype(F32).reshape(SLOTS, -1).astype(BF16)

        def add(p, carry):
            rows = pl.ds(pl.multiple_of(p * PIECE, PIECE), PIECE)
            total[rows, :] += jnp.dot(spread[rows, :], values, preferred_element_type=F32)
            return carry

        lax.fori_loop(0, nodes // PIECE, add, 0)
        return carry

    lax.fori_loop(0, GROUPS - 1, scatter, 0)

    total_copy = pltpu.make_async_copy(total, total_ref, out_sem.at[2])
    total_copy.start()
    mark_group(0)
    spread_copy = pltpu.make_async_copy(spread, spread_ref, out_sem.at[3])
    spread_copy.start()
    arrived = last_ref.at[pl.ds(1, GROUP - 1)]
    pltpu.make_async_copy(arrived, arrived, back_sem.at[0]).wait()
    pltpu.make_async_copy(recv.at[all_but_one], recv.at[all_but_one], send_sem.at[1]).wait()
    for copy in (hid_copy, bnd_copy, total_copy, spread_copy):
        copy.wait()


def finish_kernel(hid, bnd, total, spread, last, hid_out, grad_out, bnd_out, grad, sem):
    whole = [
        pltpu.make_async_copy(hid, hid_out, sem.at[0]),
        pltpu.make_async_copy(bnd, bnd_out, sem.at[1]),
    ]
    for copy in whole:
        copy.start()
    values = last[...].astype(F32).reshape(SLOTS, -1).astype(BF16)
    for p in range(grad.shape[0] // PIECE):
        rows = pl.ds(p * PIECE, PIECE)
        added = total[rows, :] + jnp.dot(spread[rows, :], values, preferred_element_type=F32)
        grad[rows, :] = added.astype(BF16)
        pltpu.make_async_copy(grad.at[rows], grad_out.at[rows], sem.at[2]).start()
    for copy in whole:
        copy.wait()
    pltpu.make_async_copy(grad, grad_out, sem.at[2]).wait()


def per_device(
    features,
    prev_features,
    cotangent,
    adjacency,
    tile_cols,
    send_idx,
    send_cnt,
    recv_cnt,
    stale_grad,
    w_self,
    w_neigh,
    layer_bias,
):
    nodes, width = features.shape
    tiles = adjacency.shape[0]
    rows = jax.ShapeDtypeStruct((nodes, width), BF16)
    slots = jax.ShapeDtypeStruct((PEERS, CAP, width), BF16)
    anywhere = pl.BlockSpec(memory_space=pl.ANY)
    vmem = pl.BlockSpec(memory_space=pltpu.VMEM)
    dma = pltpu.SemaphoreType.DMA
    whole = pltpu.VMEM((nodes, width), BF16)
    results = pl.pallas_call(
        layer_kernel,
        out_shape=[
            whole,
            pltpu.VMEM((PEERS, CAP, width), BF16),
            pltpu.VMEM((nodes, width), F32),
            pltpu.VMEM((nodes, SLOTS), BF16),
            pltpu.VMEM((GROUP, CAP, width), BF16),
        ],
        in_specs=[anywhere] * 12,
        out_specs=[anywhere] * 5,
        scratch_shapes=[
            pltpu.SMEM(tile_cols.shape, jnp.int32),
            pltpu.VMEM((CAP, PEERS), jnp.int32),
            pltpu.VMEM((1, PEERS), jnp.int32),
            pltpu.VMEM((1, PEERS), jnp.int32),
            pltpu.VMEM((1, width), F32),
            whole,
            pltpu.VMEM((nodes // BLOCK + GROUPS * GROUP_BLOCKS, BLOCK, width), BF16),
            pltpu.VMEM((nodes // BLOCK, BLOCK, width), BF16),
            pltpu.VMEM((2, nodes, width), BF16),
            pltpu.VMEM((2,) + w_self.shape, BF16),
            pltpu.VMEM((2,) + w_neigh.shape, BF16),
            pltpu.VMEM((2, 8, width), F32),
            pltpu.VMEM(adjacency.shape, BF16),
            pltpu.VMEM((PEERS, CAP, width), BF16),
            pltpu.VMEM((PEERS, CAP, width), BF16),
            pltpu.VMEM((PEERS - GROUP, CAP, width), BF16),
            whole,
            whole,
            whole,
            pltpu.VMEM((nodes, width), F32),
            pltpu.VMEM((tiles, BLOCK, width), F32),
            pltpu.VMEM((tiles, BLOCK, width), F32),
            pltpu.VMEM((nodes, SLOTS), BF16),
            pltpu.VMEM((GROUPS, 8, SLOTS), F32),
            pltpu.VMEM((8, BLOCK), jnp.int32),
            pltpu.SMEM((8, BLOCK), jnp.int32),
            dma((12,)),
            dma((2,)),
            dma,
            dma((GROUPS,)),
            dma((CHUNKS + 5,)),
            dma((CHUNKS + 5,)),
            dma((5,)),
        ],
        compiler_params=pltpu.CompilerParams(
            collective_id=0, has_side_effects=True, vmem_limit_bytes=53 << 20
        ),
    )(
        tile_cols,
        send_idx.T,
        send_cnt.reshape(1, PEERS),
        recv_cnt.reshape(1, PEERS),
        layer_bias.reshape(1, width),
        features.reshape(nodes // BLOCK, BLOCK, width),
        prev_features,
        cotangent,
        adjacency,
        stale_grad,
        w_self,
        w_neigh,
    )
    return pl.pallas_call(
        finish_kernel,
        out_shape=[rows, rows, slots],
        in_specs=[vmem] * 5,
        out_specs=[anywhere] * 3,
        scratch_shapes=[whole, dma((3,))],
        compiler_params=pltpu.CompilerParams(vmem_limit_bytes=FINISH_MB << 20),
    )(*[pltpu.with_memory_space_constraint(result, pltpu.VMEM) for result in results])


def solution(mesh):
    return jax.shard_map(
        per_device,
        mesh=mesh,
        in_specs=(
            P("dom", "feat"),
            P("dom", "feat"),
            P("dom", "feat"),
            P("dom", None, None),
            P("dom"),
            P("dom", None),
            P("dom"),
            P("dom"),
            P("dom", None, "feat"),
            P("feat", None),
            P("feat", None),
            P("feat"),
        ),
        out_specs=(P("dom", "feat"), P("dom", "feat"), P("dom", None, "feat")),
        check_vma=False,
    )
```

```python
import jax
import jax.numpy as jnp
from jax import lax
from jax.experimental import pallas as pl
from jax.experimental.pallas import tpu as pltpu
from jax.sharding import PartitionSpec as P

MESH = pl.DeviceIdType.MESH
BF16, F32 = jnp.bfloat16, jnp.float32
PEERS = 128
CAP = 24
GROUP = 16
GROUPS = PEERS // GROUP
SLOTS = GROUP * CAP
BLOCK = 128
GROUP_BLOCKS = SLOTS // BLOCK
TPR = 6
CHUNKS = 4
FINISH_MB = 6
PIECE = 256
NEAR = (0, 1, 2, 1)
HOPS = [[NEAR[(c // 4 + 2 * (c % 4)) % 4] + NEAR[c % 4] + min(z, 8 - z) for z in range(8)] for c in range(16)]
FAR_FIRST = sorted(
    ((c, dz) for c in range(16) for dz in range(8) if c or dz), key=lambda at: -HOPS[at[0]][at[1]]
)
FAR_Z = (0, 4, 3, 5, 2, 6, 1, 7)
CONTRACT_LAST = (((1,), (1,)), ((), ()))
CONTRACT_FIRST = (((0,), (0,)), ((), ()))


def torus(me, sign):
    z, x, y = lax.rem(me, 8), lax.rem(me // 8, 4), me // 32

    def column(c):
        dx = lax.rem(c, 4)
        dy = lax.rem(c // 4 + 2 * dx, 4)
        if sign < 0:
            dy, dx = 4 - dy, 4 - dx
        return (lax.rem(y + dy, 4) * 4 + lax.rem(x + dx, 4)) * 8

    return column, [lax.rem(z + 8 + sign * dz, 8) for dz in range(8)]


def layer_kernel(
    tile_hbm,
    idx_hbm,
    cnt_hbm,
    taken_hbm,
    bias_hbm,
    feat_ref,
    prev_ref,
    cot_ref,
    adj_ref,
    stale_ref,
    ws_ref,
    wn_ref,
    hid_ref,
    bnd_ref,
    total_ref,
    spread_ref,
    last_ref,
    tile_ref,
    idx_ref,
    cnt_ref,
    taken_ref,
    bias_ref,
    prev,
    comb,
    feat2,
    cot,
    ws,
    wn,
    bias,
    adj,
    out_buf,
    recv,
    back,
    agg,
    agg2,
    agg_grad,
    total,
    terms,
    sums,
    spread,
    rows_of,
    meta_v,
    meta_s,
    load_sem,
    send_sem,
    recv_sem,
    back_sem,
    pair_send,
    pair_recv,
    out_sem,
):
    me, feat = lax.axis_index("dom"), lax.axis_index("feat")
    nodes = prev.shape[0]
    chunk = nodes // CHUNKS
    blocks = nodes // BLOCK
    barrier = pltpu.get_barrier_semaphore()

    column_ahead, z_ahead = torus(me, 1)
    column_behind, z_behind = torus(me, -1)

    loads = [
        pltpu.make_async_copy(src, dst, load_sem.at[n])
        for n, (src, dst) in enumerate(
            (
                (prev_ref, prev),
                (idx_hbm, idx_ref),
                (cnt_hbm, cnt_ref),
                (tile_hbm, tile_ref),
                (taken_hbm, taken_ref),
                (bias_hbm, bias_ref),
                (feat_ref, comb.at[pl.ds(0, blocks)]),
                (adj_ref, adj),
                (cot_ref, cot.at[feat]),
                (ws_ref, ws.at[0]),
                (wn_ref, wn.at[0]),
                (stale_ref.at[me], last_ref.at[0]),
            )
        )
    ]
    for load in loads[:3]:
        load.start()
    pl.semaphore_signal(barrier, inc=1, device_id=(me, 1 - feat), device_id_type=MESH)
    columns = [column_ahead(c) for c in range(PEERS // 8)]
    for c, dz in FAR_FIRST:
        peer = columns[c] + z_ahead[dz]
        pl.semaphore_signal(barrier, inc=1, device_id=(peer, feat), device_id_type=MESH)
    for load in loads[3:]:
        load.start()
    for load in loads[1:3]:
        load.wait()

    slot_of = lax.broadcasted_iota(jnp.int32, (CAP, PEERS), 0)
    idx = jnp.where(slot_of < cnt_ref[...], idx_ref[...], -1).astype(F32)
    tiled = jnp.concatenate([idx] * GROUP, axis=0)
    lane = lax.broadcasted_iota(jnp.int32, (SLOTS, PEERS), 1)
    place = lax.broadcasted_iota(jnp.int32, (GROUP, CAP, PEERS), 0).reshape(SLOTS, PEERS)
    node = lax.broadcasted_iota(jnp.int32, (SLOTS, nodes), 1)
    loads[0].wait()

    def gather(g, carry):
        i = g * GROUP + place
        dz, dx = i & 7, (i >> 3) & 3
        dy = ((i >> 5) + 2 * dx) & 3
        z, x, y = me & 7, (me >> 3) & 3, me >> 5
        dest = (((y + dy) & 3) * 4 + ((x + dx) & 3)) * 8 + ((z + dz) & 7)
        column = jnp.sum(jnp.where(lane == dest, tiled, 0.0), axis=1, keepdims=True)
        pick = (node == column.astype(jnp.int32)).astype(F32).astype(BF16)
        sent = jnp.dot(pick, prev[...], preferred_element_type=F32)
        out_buf[pl.ds(g * GROUP, GROUP)] = sent.reshape(GROUP, CAP, -1).astype(BF16)
        rows_of[g] = jnp.transpose(jnp.broadcast_to(column, (SLOTS, PEERS)))[:8]

        @pl.when(g == 0)
        def _():
            pl.semaphore_wait(barrier, PEERS)

        def send(base, i, dz):
            pltpu.make_async_remote_copy(
                src_ref=out_buf.at[i],
                dst_ref=recv.at[me],
                send_sem=send_sem.at[0],
                recv_sem=recv_sem,
                device_id=(base + z_ahead[dz], feat),
                device_id_type=MESH,
            ).start()

        for half in range(2):
            base = column_ahead(2 * g + half)
            if half == 0:
                pl.when(g > 0)(lambda: send(base, g * GROUP, 0))
            for dz in FAR_Z[1 - half :]:
                send(base, g * GROUP + half * 8 + dz, dz)
        return carry

    lax.fori_loop(0, GROUPS, gather, 0)
    recv[me] = out_buf[0]

    def to_pair(n, src, dst):
        return pltpu.make_async_remote_copy(
            src_ref=src,
            dst_ref=dst,
            send_sem=pair_send.at[n],
            recv_sem=pair_recv.at[n],
            device_id=(me, 1 - feat),
            device_id_type=MESH,
        )

    for load in loads[3:6]:
        load.wait()
    bias[feat] = jnp.broadcast_to(bias_ref[...], bias.shape[1:])
    pairs = [
        to_pair(CHUNKS, ws_ref, ws.at[1]),
        to_pair(CHUNKS + 1, wn_ref, wn.at[1]),
        to_pair(CHUNKS + 2, bias.at[feat], bias.at[feat]),
        to_pair(CHUNKS + 3, feat_ref, feat2),
        to_pair(CHUNKS + 4, cot_ref, cot.at[feat]),
    ]
    for pair in pairs:
        pair.start()

    def send_back(c, first, into, base_slot):
        base = column_behind(c)
        for dz in FAR_Z[first:]:
            peer = base + z_behind[dz]
            pltpu.make_async_remote_copy(
                src_ref=stale_ref.at[peer],
                dst_ref=into.at[c * 8 + dz - base_slot],
                send_sem=send_sem.at[1],
                recv_sem=back_sem.at[c // 2],
                device_id=(peer, feat),
                device_id_type=MESH,
            ).start()

    def send_back_column(c, carry):
        send_back(PEERS // 8 - 1 - c, 0, back, GROUP)
        return carry

    lax.fori_loop(0, PEERS // 8 - 2, send_back_column, 0)
    send_back(1, 0, last_ref, 0)
    send_back(0, 1, last_ref, 0)

    sub = lax.broadcasted_iota(jnp.int32, (BLOCK, BLOCK), 0)
    lanes = lax.broadcasted_iota(jnp.int32, (BLOCK, BLOCK), 1)
    tiles = adj.shape[0]

    def spread_cols(t, carry):
        down, across = carry
        col = tile_ref[t]
        return jnp.where(sub == t, col, down), jnp.where(lanes == t, col, across)

    def count(hits, axis=0):
        return jnp.sum(jnp.where(hits, 1, 0), axis=axis, keepdims=True)

    far = jnp.full((BLOCK, BLOCK), 1000, jnp.int32)
    down, across = lax.fori_loop(0, tiles, spread_cols, (far, far))
    rank = count(across * BLOCK + lanes < down * BLOCK + sub, axis=1)
    at_rank = jnp.where(lanes == rank, 1, 0)
    follows = jnp.where(lanes == rank + 1, 1, 0)
    col_here = jnp.sum(down * at_rank, axis=0, keepdims=True)
    col_before = jnp.sum((down + 1) * follows, axis=0, keepdims=True)
    meta_v[...] = jnp.zeros(meta_v.shape, jnp.int32)
    meta_v[0:1, :] = jnp.sum(sub * at_rank, axis=0, keepdims=True)
    meta_v[1:2, :] = jnp.where(col_here + 1 == col_before, 1, 0)
    meta_v[2:3, :] = jnp.maximum(count(down <= lanes) - 1, 0)
    meta_v[3:4, :] = jnp.minimum(count(down == lanes), 1)
    meta_copy = pltpu.make_async_copy(meta_v, meta_s, out_sem.at[4])
    meta_copy.start()
    meta_copy.wait()

    all_but_one = pl.ds(0, PEERS - 1)
    for load in loads[6:]:
        load.wait()
    pltpu.make_async_copy(recv.at[all_but_one], recv.at[all_but_one], recv_sem).wait()

    def place_rows(g, carry):
        rows = recv[pl.ds(g * GROUP, GROUP)].astype(F32).reshape(SLOTS, -1).astype(BF16)
        comb[pl.ds(blocks + g * GROUP_BLOCKS, GROUP_BLOCKS)] = rows.reshape(GROUP_BLOCKS, BLOCK, -1)
        return carry

    lax.fori_loop(0, GROUPS, place_rows, 0)

    def rows_of_chunk(q):
        return pl.ds(pl.multiple_of(q * chunk, chunk), chunk)

    def agg_pair(q):
        return to_pair(q, agg.at[rows_of_chunk(q)], agg2.at[rows_of_chunk(q)])

    def aggregate(q, carry):
        def row_block(r, carry):
            left = jnp.concatenate([adj[r * TPR + j] for j in range(TPR)], axis=1)
            right = jnp.concatenate(
                [comb[tile_ref[r * TPR + j]] for j in range(TPR)], axis=0
            )
            summed = jnp.dot(left, right, preferred_element_type=F32)
            agg[pl.ds(pl.multiple_of(r * BLOCK, BLOCK), BLOCK)] = summed.astype(BF16)
            return carry

        per_chunk = chunk // BLOCK
        lax.fori_loop(q * per_chunk, (q + 1) * per_chunk, row_block, 0)
        agg_pair(q).start()
        return carry

    lax.fori_loop(0, CHUNKS, aggregate, 0)
    for pair in pairs:
        pair.wait()

    def dense(q, carry):
        agg_pair(q).wait()
        rows = rows_of_chunk(q)
        own = comb[pl.ds(q * (chunk // BLOCK), chunk // BLOCK)].reshape(chunk, -1)
        other = feat2[pl.ds(q * (chunk // BLOCK), chunk // BLOCK)].reshape(chunk, -1)
        neigh_grad = self_grad = None
        for j in range(2):
            cols = slice(j * 256, (j + 1) * 256)
            preact = jnp.dot(own, ws[0, :, cols], preferred_element_type=F32)
            preact += jnp.dot(other, ws[1, :, cols], preferred_element_type=F32)
            preact += jnp.dot(agg[rows, :], wn[0, :, cols], preferred_element_type=F32)
            preact += jnp.dot(agg2[rows, :], wn[1, :, cols], preferred_element_type=F32)
            preact += bias[j][0:1, :]
            pre_grad = jnp.where(preact > 0, cot[j, rows, :].astype(F32), 0.0).astype(BF16)
            cot[j, rows, :] = jnp.maximum(preact, 0.0).astype(BF16)
            part = lax.dot_general(
                pre_grad, wn[0, :, cols], CONTRACT_LAST, preferred_element_type=F32
            )
            neigh_grad = part if j == 0 else neigh_grad + part
            part = lax.dot_general(
                pre_grad, ws[0, :, cols], CONTRACT_LAST, preferred_element_type=F32
            )
            self_grad = part if j == 0 else self_grad + part
        agg_grad[rows, :] = neigh_grad.astype(BF16)
        total[rows, :] = self_grad
        return carry

    lax.fori_loop(0, CHUNKS, dense, 0)
    hid_copy = pltpu.make_async_copy(cot.at[feat], hid_ref, out_sem.at[0])
    hid_copy.start()

    def tile_terms(r, carry):
        left = jnp.concatenate([adj[r * TPR + j] for j in range(TPR)], axis=1)
        right = agg_grad[pl.ds(pl.multiple_of(r * BLOCK, BLOCK), BLOCK), :]
        part = lax.dot_general(left, right, CONTRACT_FIRST, preferred_element_type=F32)
        terms[pl.ds(r * TPR, TPR)] = part.reshape(TPR, BLOCK, -1)
        return carry

    lax.fori_loop(0, blocks, tile_terms, 0)

    def running(i, carry):
        carry = carry * meta_s[1, i].astype(F32) + terms[meta_s[0, i]]
        sums[i] = carry
        return carry

    lax.fori_loop(0, tiles, running, jnp.zeros(terms.shape[1:], F32))

    def column_sum(c):
        return sums[meta_s[2, c]] * meta_s[3, c].astype(F32)

    def add_local(c, carry):
        rows = pl.ds(pl.multiple_of(c * BLOCK, BLOCK), BLOCK)
        total[rows, :] += column_sum(c)
        return carry

    lax.fori_loop(0, blocks, add_local, 0)

    pltpu.make_async_copy(out_buf.at[all_but_one], out_buf.at[all_but_one], send_sem.at[0]).wait()
    slot = lax.broadcasted_iota(jnp.int32, (GROUP, CAP, 256), 1).reshape(SLOTS, 256).astype(F32)
    taken = jnp.broadcast_to(taken_ref[...].astype(F32), (SLOTS, PEERS))

    def boundary(g, carry):
        first = blocks + g * GROUP_BLOCKS
        rows = jnp.concatenate([column_sum(first + n) for n in range(GROUP_BLOCKS)], axis=0)
        limit = jnp.sum(
            jnp.where(lane == g * GROUP + place, taken, 0.0), axis=1, keepdims=True
        )
        rows = jnp.where(slot < limit, rows, 0.0)
        out_buf[pl.ds(g * GROUP, GROUP)] = rows.reshape(GROUP, CAP, -1).astype(BF16)
        return carry

    lax.fori_loop(0, GROUPS, boundary, 0)
    bnd_copy = pltpu.make_async_copy(out_buf, bnd_ref, out_sem.at[1])
    bnd_copy.start()

    def mark_group(g):
        row = rows_of[g][0:1, :]

        def mark(p, carry):
            at = lax.broadcasted_iota(jnp.int32, (PIECE, SLOTS), 0) + p * PIECE
            hit = jnp.where(at.astype(F32) == row, 1.0, 0.0)
            spread[pl.ds(pl.multiple_of(p * PIECE, PIECE), PIECE), :] = hit.astype(BF16)
            return carry

        lax.fori_loop(0, nodes // PIECE, mark, 0)

    def scatter(n, carry):
        g = GROUPS - 1 - n
        mark_group(g)
        arrived = back.at[pl.ds(0, GROUP)]
        pltpu.make_async_copy(arrived, arrived, back_sem.at[g]).wait()
        values = back[pl.ds((g - 1) * GROUP, GROUP)].astype(F32).reshape(SLOTS, -1).astype(BF16)

        def add(p, carry):
            rows = pl.ds(pl.multiple_of(p * PIECE, PIECE), PIECE)
            total[rows, :] += jnp.dot(spread[rows, :], values, preferred_element_type=F32)
            return carry

        lax.fori_loop(0, nodes // PIECE, add, 0)
        return carry

    lax.fori_loop(0, GROUPS - 1, scatter, 0)

    total_copy = pltpu.make_async_copy(total, total_ref, out_sem.at[2])
    total_copy.start()
    mark_group(0)
    spread_copy = pltpu.make_async_copy(spread, spread_ref, out_sem.at[3])
    spread_copy.start()
    arrived = last_ref.at[pl.ds(1, GROUP - 1)]
    pltpu.make_async_copy(arrived, arrived, back_sem.at[0]).wait()
    pltpu.make_async_copy(recv.at[all_but_one], recv.at[all_but_one], send_sem.at[1]).wait()
    for copy in (hid_copy, bnd_copy, total_copy, spread_copy):
        copy.wait()


def finish_kernel(hid, bnd, total, spread, last, hid_out, grad_out, bnd_out, grad, sem):
    whole = [
        pltpu.make_async_copy(hid, hid_out, sem.at[0]),
        pltpu.make_async_copy(bnd, bnd_out, sem.at[1]),
    ]
    for copy in whole:
        copy.start()
    values = last[...].astype(F32).reshape(SLOTS, -1).astype(BF16)
    for p in range(grad.shape[0] // PIECE):
        rows = pl.ds(p * PIECE, PIECE)
        added = total[rows, :] + jnp.dot(spread[rows, :], values, preferred_element_type=F32)
        grad[rows, :] = added.astype(BF16)
        pltpu.make_async_copy(grad.at[rows], grad_out.at[rows], sem.at[2]).start()
    for copy in whole:
        copy.wait()
    pltpu.make_async_copy(grad, grad_out, sem.at[2]).wait()


def per_device(
    features,
    prev_features,
    cotangent,
    adjacency,
    tile_cols,
    send_idx,
    send_cnt,
    recv_cnt,
    stale_grad,
    w_self,
    w_neigh,
    layer_bias,
):
    nodes, width = features.shape
    tiles = adjacency.shape[0]
    rows = jax.ShapeDtypeStruct((nodes, width), BF16)
    slots = jax.ShapeDtypeStruct((PEERS, CAP, width), BF16)
    anywhere = pl.BlockSpec(memory_space=pl.ANY)
    vmem = pl.BlockSpec(memory_space=pltpu.VMEM)
    dma = pltpu.SemaphoreType.DMA
    whole = pltpu.VMEM((nodes, width), BF16)
    results = pl.pallas_call(
        layer_kernel,
        out_shape=[
            whole,
            pltpu.VMEM((PEERS, CAP, width), BF16),
            pltpu.VMEM((nodes, width), F32),
            pltpu.VMEM((nodes, SLOTS), BF16),
            pltpu.VMEM((GROUP, CAP, width), BF16),
        ],
        in_specs=[anywhere] * 12,
        out_specs=[anywhere] * 5,
        scratch_shapes=[
            pltpu.SMEM(tile_cols.shape, jnp.int32),
            pltpu.VMEM((CAP, PEERS), jnp.int32),
            pltpu.VMEM((1, PEERS), jnp.int32),
            pltpu.VMEM((1, PEERS), jnp.int32),
            pltpu.VMEM((1, width), F32),
            whole,
            pltpu.VMEM((nodes // BLOCK + GROUPS * GROUP_BLOCKS, BLOCK, width), BF16),
            pltpu.VMEM((nodes // BLOCK, BLOCK, width), BF16),
            pltpu.VMEM((2, nodes, width), BF16),
            pltpu.VMEM((2,) + w_self.shape, BF16),
            pltpu.VMEM((2,) + w_neigh.shape, BF16),
            pltpu.VMEM((2, 8, width), F32),
            pltpu.VMEM(adjacency.shape, BF16),
            pltpu.VMEM((PEERS, CAP, width), BF16),
            pltpu.VMEM((PEERS, CAP, width), BF16),
            pltpu.VMEM((PEERS - GROUP, CAP, width), BF16),
            whole,
            whole,
            whole,
            pltpu.VMEM((nodes, width), F32),
            pltpu.VMEM((tiles, BLOCK, width), F32),
            pltpu.VMEM((tiles, BLOCK, width), F32),
            pltpu.VMEM((nodes, SLOTS), BF16),
            pltpu.VMEM((GROUPS, 8, SLOTS), F32),
            pltpu.VMEM((8, BLOCK), jnp.int32),
            pltpu.SMEM((8, BLOCK), jnp.int32),
            dma((12,)),
            dma((2,)),
            dma,
            dma((GROUPS,)),
            dma((CHUNKS + 5,)),
            dma((CHUNKS + 5,)),
            dma((5,)),
        ],
        compiler_params=pltpu.CompilerParams(
            collective_id=0, has_side_effects=True, vmem_limit_bytes=53 << 20
        ),
    )(
        tile_cols,
        send_idx.T,
        send_cnt.reshape(1, PEERS),
        recv_cnt.reshape(1, PEERS),
        layer_bias.reshape(1, width),
        features.reshape(nodes // BLOCK, BLOCK, width),
        prev_features,
        cotangent,
        adjacency,
        stale_grad,
        w_self,
        w_neigh,
    )
    return pl.pallas_call(
        finish_kernel,
        out_shape=[rows, rows, slots],
        in_specs=[vmem] * 5,
        out_specs=[anywhere] * 3,
        scratch_shapes=[whole, dma((3,))],
        compiler_params=pltpu.CompilerParams(vmem_limit_bytes=FINISH_MB << 20),
    )(*[pltpu.with_memory_space_constraint(result, pltpu.VMEM) for result in results])


def solution(mesh):
    return jax.shard_map(
        per_device,
        mesh=mesh,
        in_specs=(
            P("dom", "feat"),
            P("dom", "feat"),
            P("dom", "feat"),
            P("dom", None, None),
            P("dom"),
            P("dom", None),
            P("dom"),
            P("dom"),
            P("dom", None, "feat"),
            P("feat", None),
            P("feat", None),
            P("feat"),
        ),
        out_specs=(P("dom", "feat"), P("dom", "feat"), P("dom", None, "feat")),
        check_vma=False,
    )
```
